32 devices in a mesh: basin: 8 (over y, x, core), member: 4 (over z).
Axes of the slice: x: 2, y: 2, z: 4, core: 2. Of those that a mesh axis runs over, the one named last changes fastest.
Arguments:
- initial_reservoir_levels: float32 [64, 4, 8192], P('member', None, 'basin'), may hold values from 0 to 1
- normalized_catchment_settings: float32 [10, 8192], P(None, 'basin'), may hold values from 0 to 1
- rainfall_member_series: float32 [24, 64, 8192], P(None, 'member', 'basin'), may hold values from 0 to 0.03
- surface_heat_celsius: float32 [24, 8192], P(None, 'basin'), may hold values from -12 to 12
- potential_evapotranspiration: float32 [24, 8192], P(None, 'basin'), may hold values from 0 to 0.01
- gauge_measured_values: float32 [32, 32], P('basin'), may hold values from 0 to 1
- gauge_deviation_sigma: float32 [32, 32], P('basin'), may hold values from 0.05 to 0.5
- gauge_perturbation_draws: float32 [32, 32, 64], P('basin', None, 'member'), may hold values from -6 to 6
- gauge_catchment_position: int32 [32, 32], P('basin'), may hold values from 0 to 255
- gauge_present_flag: int32 [32, 32], P('basin'), may hold values 0 or 1
- adjacent_block_list: int32 [32, 3], replicated, may hold values from 0 to 31, as said below
Outputs:
- analysis: float32 [64, 4, 8192], P('member', None, 'basin')
- discharge_series: float32 [24, 64, 8192], P(None, 'member', 'basin')
The draws below stay inside these ranges and needn't reach their ends.
Inputs may be any that keep to these rules, and one draw needn't show every extreme that they name: `adjacent_block_list`: no block lists itself. Of the 12 entries of any aligned range of 4 blocks, at most 3 point into any one aligned range of 4 blocks, and exactly 3 into some range.
All inputs are finite; a program needn't handle non-finite values. No bound on the sum of `gauge_present_flag` on one device may be relied on, other than what follows from the above.
Results may differ from the reference program's by a relative error of at most 0.0003.
Values sent between devices are 32-bit elements; how exact they have to be, the bound alone decides.
No kernel may reach another device: no remote copies, remote signals or barrier semaphores. Data moves between devices by JAX's collectives and lax.ppermute only.
A program may use at most 64 MiB of HBM per device.

```python
import math
import jax
import jax.numpy as jnp
from jax import lax

NB = 256
BLK_DEV = 4
ENSEMBLE_SIZE = 64
LEAD_TIME_LENGTH = 24
OBS = 32
NBR = 3
NPAR = 10
LOCAL = 128
BLOCKS = 32
CATCHMENT_COUNT = 8192
CAP = 3


def draw_adjacent_block_list(key, part):
    device_count = BLOCKS // BLK_DEV
    entries = BLK_DEV * NBR
    key_shift, key_pool, key_order, key_block = jax.random.split(key, 4)
    first_shift = jax.random.randint(key_shift, (), 0, device_count)
    other_shift = (first_shift + 1 + jnp.arange(device_count - 1, dtype=jnp.int32)) % device_count
    shift_pool = jnp.repeat(other_shift, CAP)
    pool_order = jax.random.permutation(key_pool, shift_pool.shape[0])
    remaining = shift_pool[pool_order][:entries - CAP]
    shifts = jnp.concatenate([jnp.full((CAP,), first_shift, dtype=jnp.int32), remaining.astype(jnp.int32)])
    scores = jax.random.randint(key_order, (device_count, entries), 0, 1024) * entries + jnp.arange(entries, dtype=jnp.int32)[None, :]
    placed = jnp.argsort(scores, axis=1)
    device_shift = shifts[placed]
    device_ids = jnp.arange(device_count, dtype=jnp.int32)[:, None]
    owner_dev = (device_ids + device_shift) % device_count
    local_block = jax.random.randint(key_block, (device_count, entries), 0, BLK_DEV)
    home_block = jnp.arange(entries, dtype=jnp.int32)[None, :] // NBR
    clash = (owner_dev == device_ids) & (local_block == home_block)
    local_block = jnp.where(clash, (local_block + 1) % BLK_DEV, local_block)
    return (owner_dev * BLK_DEV + local_block).reshape(BLOCKS, NBR).astype(jnp.int32)


def plant(drawn, key, low, high):
    longest = drawn.shape.index(max(drawn.shape))
    spots = []
    for shift in (0, 1):
        where = [jax.random.randint(jax.random.fold_in(key, axis), (), 0, length) for axis, length in enumerate(drawn.shape)]
        where[longest] = (where[longest] + shift) % drawn.shape[longest]
        spots.append(tuple(where))
    return drawn.at[spots[0]].set(low).at[spots[1]].set(high)


def block_levels(key, dims, cuts, smallest, top_value):
    factor_of = 1.0
    for dim, parts in cuts:
        steps = jax.random.uniform(jax.random.fold_in(jax.random.fold_in(key, 6), dim), (parts,), jnp.float32, smallest / len(cuts), top_value / len(cuts))
        factor_of = factor_of * jnp.repeat(jnp.exp(steps), dims[dim] // parts).reshape((-1,) + (1,) * (len(dims) - 1 - dim))
    return factor_of


def gaussian(rng, extent, deviation, bound, cuts=(), held_as=jnp.bfloat16):
    drawn = jax.random.normal(rng, extent, jnp.float32) * deviation
    if len(cuts) > 0:
        drawn = block_levels(rng, extent, cuts, -0.22, 0.18) * drawn
    return jnp.clip(drawn, min=-bound, max=bound).astype(held_as)


def setup_inputs(seed: int = 0) -> dict:
    key_list = jax.random.split(jax.random.key(seed), 12)
    return {
        "initial_reservoir_levels": jnp.clip(1.0 * jax.random.uniform(key_list[0], (ENSEMBLE_SIZE, 4, CATCHMENT_COUNT), jnp.float32) ** block_levels(key_list[0], (ENSEMBLE_SIZE, 4, CATCHMENT_COUNT), ((0, 4), (2, 8)), -0.2, 0.2), 0.0, 1.0),
        "normalized_catchment_settings": jnp.clip(1.0 * jax.random.uniform(key_list[1], (NPAR, CATCHMENT_COUNT), jnp.float32) ** block_levels(key_list[1], (NPAR, CATCHMENT_COUNT), ((1, 8),), -0.2, 0.2), 0.0, 1.0),
        "rainfall_member_series": jnp.clip(0.03 * jax.random.uniform(key_list[2], (LEAD_TIME_LENGTH, ENSEMBLE_SIZE, CATCHMENT_COUNT), jnp.float32) ** block_levels(key_list[2], (LEAD_TIME_LENGTH, ENSEMBLE_SIZE, CATCHMENT_COUNT), ((1, 4), (2, 8)), -0.2, 0.2), 0.0, 0.03),
        "surface_heat_celsius": gaussian(key_list[3], (LEAD_TIME_LENGTH, CATCHMENT_COUNT), 4.0, 12.0, ((1, 8),), jnp.float32),
        "potential_evapotranspiration": jnp.clip(0.01 * jax.random.uniform(key_list[4], (LEAD_TIME_LENGTH, CATCHMENT_COUNT), jnp.float32) ** block_levels(key_list[4], (LEAD_TIME_LENGTH, CATCHMENT_COUNT), ((1, 8),), -0.2, 0.2), 0.0, 0.01),
        "gauge_measured_values": jnp.clip(1.0 * jax.random.uniform(key_list[5], (BLOCKS, OBS), jnp.float32) ** block_levels(key_list[5], (BLOCKS, OBS), ((0, 8),), -0.2, 0.2), 0.0, 1.0),
        "gauge_deviation_sigma": jnp.clip(jnp.exp(math.log(0.5) - 2.3025851 * jax.random.uniform(key_list[6], (BLOCKS, OBS), jnp.float32) ** block_levels(key_list[6], (BLOCKS, OBS), ((0, 8),), -0.2, 0.2)), 0.05, 0.5),
        "gauge_perturbation_draws": gaussian(key_list[7], (BLOCKS, OBS, ENSEMBLE_SIZE), 1.0, 6.0, ((0, 8), (2, 4)), jnp.float32),
        "gauge_catchment_position": plant(jax.random.randint(key_list[8], (BLOCKS, OBS), 0, NB), jax.random.fold_in(key_list[8], 1), 0, NB - 1).astype(jnp.int32),
        "gauge_present_flag": plant((jax.random.randint(key_list[9], (BLOCKS, OBS), 0, 4) < 3).astype(jnp.int32), jax.random.fold_in(key_list[9], 1), 0, 1),
        "adjacent_block_list": draw_adjacent_block_list(jax.random.fold_in(key_list[11], 71), 0),
    }


PARAM_LOW = (-1.5, 0.0002, 0.8, 1.0, 0.4, 0.01, 0.002, 0.0001, 0.1, 0.0001)
PARAM_HIGH = (1.5, 0.002, 4.0, 5.0, 1.0, 0.05, 0.02, 0.002, 0.5, 0.001)

def unpack_params(normalized_catchment_settings):
    return tuple((PARAM_LOW[k] + (PARAM_HIGH[k] - PARAM_LOW[k]) * normalized_catchment_settings[k] for k in range(10)))

def hbv_hour(reservoir_contents, forcing, hydrologic_settings):
    snowpack, moisture, upper_zone, lower_zone = reservoir_contents
    rain_in, air_temp, evap_pot = forcing
    thresh, melt_rate, field_cap, shape_exp, evap_limit, quick_rate, upper_rate, lower_rate, upper_limit, percolation = hydrologic_settings
    snow_share = jnp.clip((thresh + 1.0 - air_temp) * 0.5, 0.0, 1.0)
    snowpack = snowpack + snow_share * rain_in
    snowmelt = jnp.minimum(melt_rate * jnp.maximum(air_temp - thresh, 0.0), snowpack)
    snowpack = snowpack - snowmelt
    inflow = (1.0 - snow_share) * rain_in + snowmelt
    recharge = inflow * jnp.power(moisture / field_cap, shape_exp)
    moisture = moisture + inflow - recharge
    excess = jnp.maximum(moisture - field_cap, 0.0)
    moisture = moisture - excess
    actual = jnp.minimum(evap_pot * jnp.minimum(moisture / (evap_limit * field_cap), 1.0), moisture)
    moisture = moisture - actual
    upper_zone = upper_zone + recharge + excess
    perc_flow = jnp.minimum(percolation, upper_zone)
    upper_zone = upper_zone - perc_flow
    lower_zone = lower_zone + perc_flow
    quick_flow = quick_rate * jnp.maximum(upper_zone - upper_limit, 0.0)
    slow_flow = upper_rate * upper_zone
    base_flow = lower_rate * lower_zone
    upper_zone = upper_zone - quick_flow - slow_flow
    lower_zone = lower_zone - base_flow
    return ((snowpack, moisture, upper_zone, lower_zone), quick_flow + slow_flow + base_flow)

def predict_ensemble_discharge(initial_reservoir_levels, normalized_catchment_settings, rainfall_member_series, surface_heat_celsius, potential_evapotranspiration):
    hydrologic_settings = unpack_params(normalized_catchment_settings)
    reservoir_contents = (initial_reservoir_levels[:, 0], initial_reservoir_levels[:, 1], initial_reservoir_levels[:, 2], initial_reservoir_levels[:, 3])

    def advance_single_interval(carry, forcing):
        new_state, runoff = hbv_hour(carry, forcing, hydrologic_settings)
        return (new_state, 100.0 * runoff)
    reservoir_contents, discharge_series = lax.scan(advance_single_interval, reservoir_contents, (rainfall_member_series, surface_heat_celsius, potential_evapotranspiration))
    return (reservoir_contents, discharge_series, hydrologic_settings)

def reference(initial_reservoir_levels, normalized_catchment_settings, rainfall_member_series, surface_heat_celsius, potential_evapotranspiration, gauge_measured_values, gauge_deviation_sigma, gauge_perturbation_draws, gauge_catchment_position, gauge_present_flag, adjacent_block_list):
    highest = lax.Precision.HIGHEST
    reservoir_contents, discharge_series, hydrologic_settings = predict_ensemble_discharge(initial_reservoir_levels, normalized_catchment_settings, rainfall_member_series, surface_heat_celsius, potential_evapotranspiration)
    snowpack, moisture, upper_zone, lower_zone = reservoir_contents
    members = moisture.shape[0]
    blocks = gauge_measured_values.shape[0]
    wetness = 0.45 * moisture / hydrologic_settings[2]
    slot_gauge = jnp.arange(OBS) < OBS // 2

    def pick(field):
        grid = field.reshape(members, blocks, NB)
        return jnp.take_along_axis(grid, gauge_catchment_position[None], axis=2)
    predicted = jnp.where(slot_gauge, pick(discharge_series[-1]), pick(wetness))
    predicted = jnp.transpose(predicted, (1, 2, 0))
    perturbed = gauge_measured_values[..., None] + gauge_deviation_sigma[..., None] * gauge_perturbation_draws
    avail = gauge_present_flag.astype(jnp.float32)

    def localize(table):
        joined = jnp.concatenate([table[:, None], table[adjacent_block_list]], axis=1)
        return joined.reshape((blocks, LOCAL) + table.shape[2:])
    local_pred = localize(predicted)
    local_pert = localize(perturbed)
    local_sd = localize(gauge_deviation_sigma)
    local_avail = localize(avail)
    anomaly = local_avail[..., None] * (local_pred - jnp.mean(local_pred, axis=2, keepdims=True))
    innovation = local_avail[..., None] * (local_pert - local_pred)
    state_rows = jnp.concatenate([moisture.reshape(members, blocks, NB), upper_zone.reshape(members, blocks, NB)], axis=2)
    state_rows = jnp.transpose(state_rows, (1, 2, 0))
    state_anom = state_rows - jnp.mean(state_rows, axis=2, keepdims=True)
    scale = 1.0 / (members - 1)
    obs_cov = jnp.einsum('blm,bkm->blk', anomaly, anomaly, precision=highest) * scale
    obs_cov = obs_cov + local_sd[:, :, None] ** 2 * jnp.eye(LOCAL, dtype=jnp.float32)
    cross = jnp.einsum('brm,blm->brl', state_anom, anomaly, precision=highest) * scale
    factor = jnp.linalg.cholesky(obs_cov)
    weights = jax.vmap(lambda lower_tri, rhs: jax.scipy.linalg.cho_solve((lower_tri, True), rhs))(factor, innovation)
    updated = state_rows + jnp.einsum('brl,blm->brm', cross, weights, precision=highest)
    updated = jnp.transpose(updated, (2, 0, 1))
    moisture_new = updated[..., :NB].reshape(members, -1)
    upper_new = updated[..., NB:].reshape(members, -1)
    analysis = jnp.stack([snowpack, moisture_new, upper_new, lower_zone], axis=1)
    return (analysis, discharge_series)
```

```python
import functools

import jax
import jax.numpy as jnp
from jax import lax
from jax.experimental import pallas as pl
from jax.experimental.pallas import tpu as pltpu
from jax.sharding import PartitionSpec as P

NB = 256
OBS = 32
NBR = 3
LOCAL = 128

PARAM_LOW = (-1.5, 0.0002, 0.8, 1.0, 0.4, 0.01, 0.002, 0.0001, 0.1, 0.0001)
PARAM_HIGH = (1.5, 0.002, 4.0, 5.0, 1.0, 0.05, 0.02, 0.002, 0.5, 0.001)

HIGHEST = lax.Precision.HIGHEST
STRIP = 512
CHUNK = 6
PACK = 40
VMEM_LIMIT = 48 * 1024 * 1024


def lanes_of(table):
    return jnp.concatenate([table[b : b + 1] for b in range(table.shape[0])], axis=1)


def three_parts(x):
    high = x.astype(jnp.bfloat16)
    rest = x - high.astype(jnp.float32)
    middle = rest.astype(jnp.bfloat16)
    low = (rest - middle.astype(jnp.float32)).astype(jnp.bfloat16)
    return [high, middle, low]


def forecast_kernel(
    levels,
    settings,
    rain_hbm,
    heat,
    evap,
    measured,
    sigma,
    draws,
    position,
    present,
    flow_hbm,
    wet_state,
    dry_state,
    pack,
    rain,
    flow,
    share,
    melt_cap,
    last_flow,
    in_sems,
    out_sems,
):
    hours, members, width = rain_hbm.shape
    strip = min(STRIP, width)
    pieces = [(s, c) for s in range(width // strip) for c in range(hours // CHUNK)]

    def part(s, c):
        return (pl.ds(c * CHUNK, CHUNK), slice(None), pl.ds(s * strip, strip))

    def rain_copy(n):
        where = part(*pieces[n])
        return pltpu.make_async_copy(rain_hbm.at[where], rain.at[where], in_sems.at[n])

    def flow_copy(n):
        where = part(*pieces[n])
        return pltpu.make_async_copy(flow.at[where], flow_hbm.at[where], out_sems.at[n])

    for n in range(len(pieces)):
        rain_copy(n).start()

    def parameter(k, where=slice(None)):
        return PARAM_LOW[k] + (PARAM_HIGH[k] - PARAM_LOW[k]) * settings[k : k + 1, where]

    share[...] = jnp.clip((parameter(0) + 1.0 - heat[...]) * 0.5, 0.0, 1.0)
    melt_cap[...] = parameter(1) * jnp.maximum(heat[...] - parameter(0), 0.0)

    for s in range(width // strip):
        where = pl.ds(s * strip, strip)
        field_cap = parameter(2, where)
        inv_cap = 1.0 / field_cap
        shape_exp = parameter(3, where)
        inv_limit = 1.0 / (parameter(4, where) * field_cap)
        quick_rate, upper_rate, lower_rate, upper_limit, percolation = (
            parameter(k, where) for k in range(5, 10)
        )
        state = tuple(levels[:, k, where] for k in range(4))

        def hour(h, state):
            snow, moist, upper, lower = state
            fall = rain[h, :, where]
            snow_fall = share[pl.ds(h, 1), where] * fall
            snow = snow + snow_fall
            melt = jnp.minimum(melt_cap[pl.ds(h, 1), where], snow)
            snow = snow - melt
            inflow = (fall - snow_fall) + melt
            recharge = inflow * jnp.exp2(shape_exp * jnp.log2(moist * inv_cap))
            moist = moist + inflow - recharge
            excess = jnp.maximum(moist - field_cap, 0.0)
            moist = moist - excess
            actual = jnp.minimum(
                evap[pl.ds(h, 1), where] * jnp.minimum(moist * inv_limit, 1.0), moist
            )
            moist = moist - actual
            upper = upper + recharge + excess
            perc_flow = jnp.minimum(percolation, upper)
            upper = upper - perc_flow
            lower = lower + perc_flow
            fast = quick_rate * jnp.maximum(upper - upper_limit, 0.0) + upper_rate * upper
            base = lower_rate * lower
            upper = upper - fast
            lower = lower - base
            flow[h, :, where] = 100.0 * (fast + base)
            return (snow, moist, upper, lower)

        for c in range(hours // CHUNK):
            n = s * (hours // CHUNK) + c
            rain_copy(n).wait()
            state = lax.fori_loop(c * CHUNK, (c + 1) * CHUNK, hour, state, unroll=2)
            flow_copy(n).start()
        snow, moist, upper, lower = state
        wet_state[0, :, where] = moist
        wet_state[1, :, where] = upper
        dry_state[0, :, where] = snow
        dry_state[1, :, where] = lower
        last_flow[:, where] = 0.45 * moist * inv_cap

    slots = lanes_of(position[...])
    pick = (lax.broadcasted_iota(jnp.int32, (NB, LOCAL), 0) == slots).astype(jnp.bfloat16)
    blocks = width // NB
    fields = []
    for b in range(blocks):
        where = pl.ds(b * NB, NB)
        fields += three_parts(flow[hours - 1, :, where]) + three_parts(last_flow[:, where])
    taken = jnp.dot(jnp.concatenate(fields, axis=0), pick, preferred_element_type=jnp.float32)
    lane = lax.broadcasted_iota(jnp.int32, (members, LOCAL), 1)
    predicted = jnp.zeros((members, LOCAL), jnp.float32)
    for b in range(blocks):
        part6 = [taken[(b * 6 + k) * members : (b * 6 + k + 1) * members] for k in range(6)]
        gauge = (part6[2] + part6[1]) + part6[0]
        smap = (part6[5] + part6[4]) + part6[3]
        chosen = jnp.where(lane % OBS < OBS // 2, gauge, smap)
        predicted = jnp.where(lane // OBS == b, chosen, predicted)
    sd = lanes_of(sigma[...])
    spread = jnp.transpose(draws[...].reshape(LOCAL, members))
    pack[0:members] = predicted
    pack[members : 2 * members] = lanes_of(measured[...]) + sd * spread
    tail = pack.shape[0] - 2 * members
    pack[2 * members :] = jnp.broadcast_to(
        lanes_of(present[...].astype(jnp.float32)) / sd, (tail, LOCAL)
    )
    for n in range(len(pieces)):
        flow_copy(n).wait()


def forecast(levels, settings, rain, heat, evap, measured, sigma, draws, position, present):
    hours, members, width = rain.shape
    copies = (width // min(STRIP, width)) * (hours // CHUNK)
    f32 = jnp.float32
    vmem = pl.BlockSpec(memory_space=pltpu.VMEM)
    hbm = pl.BlockSpec(memory_space=pl.ANY)
    return pl.pallas_call(
        forecast_kernel,
        out_shape=(
            jax.ShapeDtypeStruct((hours, members, width), f32),
            jax.ShapeDtypeStruct((2, members, width), f32),
            jax.ShapeDtypeStruct((2, members, width), f32),
            jax.ShapeDtypeStruct((2 * members + 8, LOCAL), f32),
        ),
        in_specs=[vmem, vmem, hbm] + [vmem] * 7,
        out_specs=(hbm, vmem, vmem, vmem),
        scratch_shapes=[
            pltpu.VMEM((hours, members, width), f32),
            pltpu.VMEM((hours, members, width), f32),
            pltpu.VMEM((hours, width), f32),
            pltpu.VMEM((hours, width), f32),
            pltpu.VMEM((members, width), f32),
            pltpu.SemaphoreType.DMA((copies,)),
            pltpu.SemaphoreType.DMA((copies,)),
        ],
        compiler_params=pltpu.CompilerParams(vmem_limit_bytes=VMEM_LIMIT),
        name="forecast",
    )(levels, settings, rain, heat, evap, measured, sigma, draws, position, present)


def localize_kernel(relative, count, index, adjacency, *refs):
    pieces, (pred_out, innov_out, weight_out, table) = refs[:count], refs[count:]
    at = 0
    for piece in pieces:
        n = piece.shape[0] if len(piece.shape) == 3 else 1
        table[at : at + n] = piece[...].reshape((n,) + table.shape[1:])
        at += n
    me = index[0]
    blocks, members, _ = pred_out.shape
    rows = table.shape[1]
    lane = lax.broadcasted_iota(jnp.int32, (rows, LOCAL), 1) // OBS
    for b in range(blocks):
        local = jnp.zeros((rows, LOCAL), jnp.float32)
        for i in range(NBR + 1):
            source = me * blocks + b if i == 0 else adjacency[me * blocks + b, i - 1]
            owner = source // blocks
            if relative:
                owner = owner ^ me
            shift = ((i + blocks - source % blocks) % blocks) * OBS
            local = jnp.where(lane == i, pltpu.roll(table[owner], shift, 1), local)
        weight = local[2 * members : 2 * members + 1]
        pred_out[b] = local[:members]
        innov_out[b] = weight * (local[members : 2 * members] - local[:members])
        weight_out[b] = weight


def localize(pieces, relative, index, adjacency, blocks, members):
    f32 = jnp.float32
    rows = 2 * members + 8
    total = sum(p.shape[0] if p.ndim == 3 else 1 for p in pieces)
    vmem = pl.BlockSpec(memory_space=pltpu.VMEM)
    smem = pl.BlockSpec(memory_space=pltpu.SMEM)
    return pl.pallas_call(
        functools.partial(localize_kernel, relative, len(pieces)),
        out_shape=(
            jax.ShapeDtypeStruct((blocks, members, LOCAL), f32),
            jax.ShapeDtypeStruct((blocks, members, LOCAL), f32),
            jax.ShapeDtypeStruct((blocks, 1, LOCAL), f32),
        ),
        in_specs=[smem, smem] + [vmem] * len(pieces),
        out_specs=(vmem, vmem, vmem),
        scratch_shapes=[pltpu.VMEM((total, rows, LOCAL), f32)],
        name="localize",
    )(index, adjacency, *pieces)


def eliminate(systems):
    size = systems[0][0].shape[0]
    groups = size // 8
    sub = lax.broadcasted_iota(jnp.int32, (8, LOCAL), 0)
    mats = [[m[g * 8 : g * 8 + 8] for g in range(groups)] for (m,) in systems]
    for k in range(size):
        home, at = divmod(k, 8)
        for mat in mats:
            columns = [jnp.broadcast_to(part[:, k : k + 1], (8, LOCAL)) for part in mat]
            pivot = jnp.broadcast_to(columns[home][at : at + 1], (8, LOCAL))
            row = jnp.broadcast_to(mat[home][at : at + 1], (8, LOCAL)) / pivot
            for g in range(groups):
                part = mat[g] - columns[g] * row
                mat[g] = jnp.where(sub == at, row, part) if g == home else part
    return [jnp.concatenate(mat, axis=0) for mat in mats]


def update_kernel(count, *refs):
    innov, weight, wet_own, dry = refs[:4]
    preds, wets = refs[4 : 4 + count], refs[4 + count : 4 + 2 * count]
    analysis = refs[-1]
    blocks, members, _ = innov.shape
    systems = []
    for b in range(blocks):
        pred = jnp.concatenate([p[b] if len(p.shape) == 3 else p[:, b].reshape(-1, LOCAL) for p in preds], axis=0)
        total = pred.shape[0]
        scaled = (pred - jnp.mean(pred, axis=0, keepdims=True)) * weight[b]
        both = jnp.concatenate(
            [scaled, innov[b], jnp.zeros((LOCAL - total - members, LOCAL), jnp.float32)], axis=0
        )
        matrix = lax.dot_general(
            scaled, both, (((1,), (1,)), ((), ())), precision=HIGHEST, preferred_element_type=jnp.float32
        )
        rows = lax.broadcasted_iota(jnp.int32, (total, LOCAL), 0)
        cols = lax.broadcasted_iota(jnp.int32, (total, LOCAL), 1)
        systems.append((matrix + jnp.where(rows == cols, float(total - 1), 0.0),))
    solved = eliminate(systems)
    for b in range(blocks):
        where = pl.ds(b * NB, NB)
        gain = solved[b]
        gain = gain - jnp.mean(gain, axis=0, keepdims=True)
        turned = jnp.transpose(gain)[total : total + members]
        for k, slot in ((0, 1), (1, 2)):
            states = jnp.concatenate(
                [w[k, :, where] if len(w.shape) == 3 else w[:, k, :, where].reshape(-1, NB) for w in wets], axis=0
            )
            analysis[:, slot, where] = wet_own[k, :, where] + jnp.dot(
                turned, states, precision=HIGHEST, preferred_element_type=jnp.float32
            )
    analysis[:, 0, :] = dry[0]
    analysis[:, 3, :] = dry[1]


def update(innov, weight, wet, dry, preds, wets):
    _, members, width = wet.shape
    vmem = pl.BlockSpec(memory_space=pltpu.VMEM)
    count = len(preds)
    return pl.pallas_call(
        functools.partial(update_kernel, count),
        out_shape=jax.ShapeDtypeStruct((members, 4, width), jnp.float32),
        in_specs=[vmem] * (4 + 2 * count),
        out_specs=vmem,
        compiler_params=pltpu.CompilerParams(vmem_limit_bytes=VMEM_LIMIT),
        name="update",
    )(innov, weight, wet, dry, *preds, *wets)


def exchange(x, axis, limit=8):
    size = lax.axis_size(axis)
    if size > limit:
        return [lax.all_gather(x, axis, axis=0, tiled=False)], False
    others = [
        lax.ppermute(x, axis, [(i, i ^ s) for i in range(size)]) for s in range(1, size)
    ]
    return [x] + others, True


def on_device(
    initial_reservoir_levels,
    normalized_catchment_settings,
    rainfall_member_series,
    surface_heat_celsius,
    potential_evapotranspiration,
    gauge_measured_values,
    gauge_deviation_sigma,
    gauge_perturbation_draws,
    gauge_catchment_position,
    gauge_present_flag,
    adjacent_block_list,
):
    members = rainfall_member_series.shape[1]
    blocks = gauge_measured_values.shape[0]
    discharge, wet, dry, pack = forecast(
        initial_reservoir_levels,
        normalized_catchment_settings,
        rainfall_member_series,
        surface_heat_celsius,
        potential_evapotranspiration,
        gauge_measured_values,
        gauge_deviation_sigma,
        gauge_perturbation_draws,
        gauge_catchment_position,
        gauge_present_flag,
    )
    index = jnp.full((1,), lax.axis_index("basin"), jnp.int32)
    packs, relative = exchange(pack, "basin")
    pred, innov, weight = localize(packs, relative, index, adjacent_block_list, blocks, members)
    preds, _ = exchange(pred, "member", 4)
    wets, _ = exchange(wet, "member", 4)
    analysis = update(innov, weight, wet, dry, preds, wets)
    return (analysis, discharge)


def solution(mesh):
    placed = (
        P("member", None, "basin"),
        P(None, "basin"),
        P(None, "member", "basin"),
        P(None, "basin"),
        P(None, "basin"),
        P("basin", None),
        P("basin", None),
        P("basin", None, "member"),
        P("basin", None),
        P("basin", None),
        P(),
    )
    return jax.shard_map(
        on_device,
        mesh=mesh,
        in_specs=placed,
        out_specs=(P("member", None, "basin"), P(None, "member", "basin")),
        check_vma=False,
    )
```

```python
import functools

import jax
import jax.numpy as jnp
from jax import lax
from jax.experimental import pallas as pl
from jax.experimental.pallas import tpu as pltpu
from jax.sharding import PartitionSpec as P

NB = 256
OBS = 32
NBR = 3
LOCAL = 128

PARAM_LOW = (-1.5, 0.0002, 0.8, 1.0, 0.4, 0.01, 0.002, 0.0001, 0.1, 0.0001)
PARAM_HIGH = (1.5, 0.002, 4.0, 5.0, 1.0, 0.05, 0.02, 0.002, 0.5, 0.001)

HIGHEST = lax.Precision.HIGHEST
STRIP = 512
CHUNK = 6
PACK = 40
VMEM_LIMIT = 16 * 1024 * 1024


def lanes_of(table):
    return jnp.concatenate([table[b : b + 1] for b in range(table.shape[0])], axis=1)


def three_parts(x):
    high = x.astype(jnp.bfloat16)
    rest = x - high.astype(jnp.float32)
    middle = rest.astype(jnp.bfloat16)
    low = (rest - middle.astype(jnp.float32)).astype(jnp.bfloat16)
    return [high, middle, low]


def forecast_kernel(*refs):
    inputs, (flow_hbm, wet_state, dry_state, pack) = refs[:10], refs[10:14]
    held, (flow, share, melt_cap, last_flow, held_sems, in_sems, out_sems) = refs[14:24], refs[24:]
    levels, settings, rain, heat, evap, measured, sigma, draws, position, present = held
    rain_hbm = inputs[2]
    hours, members, width = rain.shape
    strip = min(STRIP, width)
    pieces = [(s, c) for s in range(width // strip) for c in range(hours // CHUNK)]

    def part(s, c):
        return (pl.ds(c * CHUNK, CHUNK), slice(None), pl.ds(s * strip, strip))

    def whole_copy(k):
        return pltpu.make_async_copy(inputs[k], held[k], held_sems.at[k])

    def rain_copy(n):
        where = part(*pieces[n])
        return pltpu.make_async_copy(rain_hbm.at[where], rain.at[where], in_sems.at[n])

    def flow_copy(n):
        where = part(*pieces[n])
        return pltpu.make_async_copy(flow.at[where], flow_hbm.at[where], out_sems.at[n])

    for k in (1, 3, 4, 0):
        whole_copy(k).start()
    for n in range(len(pieces)):
        rain_copy(n).start()
    for k in range(5, 10):
        whole_copy(k).start()

    def parameter(k, where=slice(None)):
        return PARAM_LOW[k] + (PARAM_HIGH[k] - PARAM_LOW[k]) * settings[k : k + 1, where]

    whole_copy(1).wait()
    whole_copy(3).wait()
    share[...] = jnp.clip((parameter(0) + 1.0 - heat[...]) * 0.5, 0.0, 1.0)
    melt_cap[...] = parameter(1) * jnp.maximum(heat[...] - parameter(0), 0.0)
    whole_copy(4).wait()
    whole_copy(0).wait()

    for s in range(width // strip):
        where = pl.ds(s * strip, strip)
        field_cap = parameter(2, where)
        inv_cap = 1.0 / field_cap
        shape_exp = parameter(3, where)
        inv_limit = 1.0 / (parameter(4, where) * field_cap)
        quick_rate, upper_rate, lower_rate, upper_limit, percolation = (
            parameter(k, where) for k in range(5, 10)
        )
        state = tuple(levels[:, k, where] for k in range(4))

        def hour(h, state):
            snow, moist, upper, lower = state
            fall = rain[h, :, where]
            snow_fall = share[pl.ds(h, 1), where] * fall
            snow = snow + snow_fall
            melt = jnp.minimum(melt_cap[pl.ds(h, 1), where], snow)
            snow = snow - melt
            inflow = (fall - snow_fall) + melt
            recharge = inflow * jnp.exp2(shape_exp * jnp.log2(moist * inv_cap))
            moist = moist + inflow - recharge
            excess = jnp.maximum(moist - field_cap, 0.0)
            moist = moist - excess
            actual = jnp.minimum(
                evap[pl.ds(h, 1), where] * jnp.minimum(moist * inv_limit, 1.0), moist
            )
            moist = moist - actual
            upper = upper + recharge + excess
            perc_flow = jnp.minimum(percolation, upper)
            upper = upper - perc_flow
            lower = lower + perc_flow
            fast = quick_rate * jnp.maximum(upper - upper_limit, 0.0) + upper_rate * upper
            base = lower_rate * lower
            upper = upper - fast
            lower = lower - base
            flow[h, :, where] = 100.0 * (fast + base)
            return (snow, moist, upper, lower)

        for c in range(hours // CHUNK):
            n = s * (hours // CHUNK) + c
            rain_copy(n).wait()
            state = lax.fori_loop(c * CHUNK, (c + 1) * CHUNK, hour, state, unroll=2)
            flow_copy(n).start()
        snow, moist, upper, lower = state
        wet_state[0, :, where] = moist
        wet_state[1, :, where] = upper
        dry_state[0, :, where] = snow
        dry_state[1, :, where] = lower
        last_flow[:, where] = 0.45 * moist * inv_cap

    for k in range(5, 10):
        whole_copy(k).wait()
    slots = lanes_of(position[...])
    pick = (lax.broadcasted_iota(jnp.int32, (NB, LOCAL), 0) == slots).astype(jnp.bfloat16)
    blocks = width // NB
    fields = []
    for b in range(blocks):
        where = pl.ds(b * NB, NB)
        fields += three_parts(flow[hours - 1, :, where]) + three_parts(last_flow[:, where])
    taken = jnp.dot(jnp.concatenate(fields, axis=0), pick, preferred_element_type=jnp.float32)
    lane = lax.broadcasted_iota(jnp.int32, (members, LOCAL), 1)
    predicted = jnp.zeros((members, LOCAL), jnp.float32)
    for b in range(blocks):
        part6 = [taken[(b * 6 + k) * members : (b * 6 + k + 1) * members] for k in range(6)]
        gauge = (part6[2] + part6[1]) + part6[0]
        smap = (part6[5] + part6[4]) + part6[3]
        chosen = jnp.where(lane % OBS < OBS // 2, gauge, smap)
        predicted = jnp.where(lane // OBS == b, chosen, predicted)
    sd = lanes_of(sigma[...])
    spread = jnp.concatenate([draws[b] for b in range(blocks)], axis=1)
    pack[0:members] = predicted
    pack[members : 2 * members] = lanes_of(measured[...]) + sd * spread
    tail = pack.shape[0] - 2 * members
    pack[2 * members :] = jnp.broadcast_to(
        lanes_of(present[...].astype(jnp.float32)) / sd, (tail, LOCAL)
    )
    for n in range(len(pieces)):
        flow_copy(n).wait()


def forecast(*arrays):
    hours, members, width = arrays[2].shape
    copies = (width // min(STRIP, width)) * (hours // CHUNK)
    f32 = jnp.float32
    vmem = pl.BlockSpec(memory_space=pltpu.VMEM)
    hbm = pl.BlockSpec(memory_space=pltpu.HBM)
    return pl.pallas_call(
        forecast_kernel,
        out_shape=(
            jax.ShapeDtypeStruct((hours, members, width), f32),
            jax.ShapeDtypeStruct((2, members, width), f32),
            jax.ShapeDtypeStruct((2, members, width), f32),
            jax.ShapeDtypeStruct((2 * members + 8, LOCAL), f32),
        ),
        in_specs=[hbm] * len(arrays),
        out_specs=(hbm, vmem, vmem, vmem),
        scratch_shapes=[pltpu.VMEM(x.shape, x.dtype) for x in arrays]
        + [
            pltpu.VMEM((hours, members, width), f32),
            pltpu.VMEM((hours, width), f32),
            pltpu.VMEM((hours, width), f32),
            pltpu.VMEM((members, width), f32),
            pltpu.SemaphoreType.DMA((len(arrays),)),
            pltpu.SemaphoreType.DMA((copies,)),
            pltpu.SemaphoreType.DMA((copies,)),
        ],
        compiler_params=pltpu.CompilerParams(vmem_limit_bytes=VMEM_LIMIT),
        name="forecast",
    )(*(pltpu.with_memory_space_constraint(x, pltpu.HBM) for x in arrays))


def localize_kernel(relative, count, index, adjacency, *refs):
    pieces, (pred_out, innov_out, weight_out, table) = refs[:count], refs[count:]
    at = 0
    for piece in pieces:
        n = piece.shape[0]
        table[at : at + n] = piece[...]
        at += n
    me = index[0]
    blocks, members, _ = pred_out.shape
    rows = table.shape[1]
    lane = lax.broadcasted_iota(jnp.int32, (rows, LOCAL), 1) // OBS
    for b in range(blocks):
        local = jnp.zeros((rows, LOCAL), jnp.float32)
        for i in range(NBR + 1):
            source = me * blocks + b if i == 0 else adjacency[i - 1, me * blocks + b]
            owner = source // blocks
            if relative:
                owner = owner ^ me
            shift = ((i + blocks - source % blocks) % blocks) * OBS
            local = jnp.where(lane == i, pltpu.roll(table[owner], shift, 1), local)
        weight = local[2 * members : 2 * members + 1]
        pred_out[b] = local[:members]
        innov_out[b] = weight * (local[members : 2 * members] - local[:members])
        weight_out[b] = weight


def localize(pieces, relative, index, adjacency, blocks, members):
    f32 = jnp.float32
    rows = 2 * members + 8
    total = sum(p.shape[0] for p in pieces)
    vmem = pl.BlockSpec(memory_space=pltpu.VMEM)
    smem = pl.BlockSpec(memory_space=pltpu.SMEM)
    return pl.pallas_call(
        functools.partial(localize_kernel, relative, len(pieces)),
        out_shape=(
            jax.ShapeDtypeStruct((blocks, members, LOCAL), f32),
            jax.ShapeDtypeStruct((blocks, members, LOCAL), f32),
            jax.ShapeDtypeStruct((blocks, 1, LOCAL), f32),
        ),
        in_specs=[smem, smem] + [vmem] * len(pieces),
        out_specs=(vmem, vmem, vmem),
        scratch_shapes=[pltpu.VMEM((total, rows, LOCAL), f32)],
        compiler_params=pltpu.CompilerParams(vmem_limit_bytes=VMEM_LIMIT),
        name="localize",
    )(index, adjacency, *pieces)


def spread_lane(x, k):
    return jnp.broadcast_to(x[:, k : k + 1], (8, LOCAL))


def spread_row(x, k):
    return jnp.broadcast_to(x[k : k + 1], (8, LOCAL))


def reduce_rows(rows, first):
    sub = lax.broadcasted_iota(jnp.int32, (8, LOCAL), 0)
    columns = [spread_lane(rows, first + j) for j in range(8)]
    for j in range(8):
        inverse = 1.0 / spread_row(columns[j], j)
        for i in range(j + 1, 8):
            scaled = spread_row(columns[i], j) * inverse
            columns[i] = jnp.where(sub == j, scaled, columns[i] - columns[j] * scaled)
        scaled = spread_row(rows, j) * inverse
        rows = jnp.where(sub == j, scaled, rows - columns[j] * scaled)
    return rows


def solve(systems):
    size = systems[0].shape[0]
    half = size // 2
    groups = half // 8

    def reduce_half(mats, first):
        mats = [[m[g * 8 : g * 8 + 8] for g in range(groups)] for m in mats]
        for p in range(groups):
            for mat in mats:
                at = first + p * 8
                mat[p] = reduce_rows(mat[p], at)
                rows = [spread_row(mat[p], j) for j in range(8)]
                for g in range(groups):
                    if g != p:
                        terms = [spread_lane(mat[g], at + j) * rows[j] for j in range(8)]
                        while len(terms) > 1:
                            terms = [terms[i] + terms[i + 1] for i in range(0, len(terms), 2)]
                        mat[g] = mat[g] - terms[0]
        return [jnp.concatenate(mat, axis=0) for mat in mats]

    def minus(x, left, right):
        return x - jnp.dot(left, right, precision=HIGHEST, preferred_element_type=jnp.float32)

    tops = reduce_half([m[:half] for m in systems], 0)
    lows = [minus(m[half:], m[half:, :half], top) for m, top in zip(systems, tops)]
    lows = reduce_half(lows, half)
    tops = [minus(top, top[:, half:size], low) for top, low in zip(tops, lows)]
    return [jnp.concatenate([top, low], axis=0) for top, low in zip(tops, lows)]


def update_kernel(count, others, *refs):
    innov, weight, wet_own, dry = refs[:4]
    preds, wets = refs[4 : 4 + count], refs[4 + count : 4 + count + others]
    analysis_hbm, analysis, out_sems = refs[4 + count + others :]
    blocks, members, _ = innov.shape

    def out_copy(b):
        where = (slice(None), slice(None), pl.ds(b * NB, NB))
        return pltpu.make_async_copy(analysis.at[where], analysis_hbm.at[where], out_sems.at[b])

    systems = []
    for b in range(blocks):
        pred = jnp.concatenate(
            [p[b] if len(p.shape) == 3 else p[:, b].reshape(-1, LOCAL) for p in preds], axis=0
        )
        total = pred.shape[0]
        scaled = (pred - jnp.mean(pred, axis=0, keepdims=True)) * weight[b]
        both = jnp.concatenate(
            [scaled, innov[b], jnp.zeros((LOCAL - total - members, LOCAL), jnp.float32)], axis=0
        )
        matrix = lax.dot_general(
            scaled,
            both,
            (((1,), (1,)), ((), ())),
            precision=HIGHEST,
            preferred_element_type=jnp.float32,
        )
        rows = lax.broadcasted_iota(jnp.int32, (total, LOCAL), 0)
        cols = lax.broadcasted_iota(jnp.int32, (total, LOCAL), 1)
        systems.append(matrix + jnp.where(rows == cols, float(total - 1), 0.0))
    solved = solve(systems)
    analysis[:, 0, :] = dry[0]
    analysis[:, 3, :] = dry[1]
    for b in range(blocks):
        where = pl.ds(b * NB, NB)
        gain = solved[b]
        gain = gain - jnp.mean(gain, axis=0, keepdims=True)
        turned = jnp.transpose(gain)[total : total + members]
        for k, slot in ((0, 1), (1, 2)):
            if len(wets[0].shape) == 3:
                states = [wet_own[k, :, where]] + [w[k, :, where] for w in wets]
            else:
                states = [w[:, k, :, where].reshape(-1, NB) for w in wets]
            analysis[:, slot, where] = wet_own[k, :, where] + jnp.dot(
                turned,
                jnp.concatenate(states, axis=0),
                precision=HIGHEST,
                preferred_element_type=jnp.float32,
            )
        out_copy(b).start()
    for b in range(blocks):
        out_copy(b).wait()


def update(innov, weight, wet, dry, preds, wets):
    _, members, width = wet.shape
    vmem = pl.BlockSpec(memory_space=pltpu.VMEM)
    hbm = pl.BlockSpec(memory_space=pltpu.HBM)
    return pl.pallas_call(
        functools.partial(update_kernel, len(preds), len(wets)),
        out_shape=jax.ShapeDtypeStruct((members, 4, width), jnp.float32),
        in_specs=[vmem] * (4 + len(preds) + len(wets)),
        out_specs=hbm,
        scratch_shapes=[
            pltpu.VMEM((members, 4, width), jnp.float32),
            pltpu.SemaphoreType.DMA((width // NB,)),
        ],
        compiler_params=pltpu.CompilerParams(vmem_limit_bytes=VMEM_LIMIT),
        name="update",
    )(innov, weight, wet, dry, *preds, *wets)


def permute(x, axis, mask):
    return lax.ppermute(x, axis, [(i, i ^ mask) for i in range(lax.axis_size(axis))])


def over_members(x):
    size = lax.axis_size("member")
    if size > 4:
        return [lax.all_gather(x, "member", axis=0)]
    return [permute(x, "member", mask) for mask in range(1, size)]


def over_basins(pack):
    size = lax.axis_size("basin")
    if size > 8:
        return [lax.all_gather(pack, "basin", axis=0)], False
    pair = jnp.stack([pack, permute(pack, "basin", 1)])
    return [pair] + [permute(pair, "basin", mask) for mask in range(2, size, 2)], True


def on_device(
    initial_reservoir_levels,
    normalized_catchment_settings,
    rainfall_member_series,
    surface_heat_celsius,
    potential_evapotranspiration,
    gauge_measured_values,
    gauge_deviation_sigma,
    gauge_perturbation_draws,
    gauge_catchment_position,
    gauge_present_flag,
    adjacent_block_list,
):
    members = rainfall_member_series.shape[1]
    blocks = gauge_measured_values.shape[0]
    discharge, wet, dry, pack = forecast(
        initial_reservoir_levels,
        normalized_catchment_settings,
        rainfall_member_series,
        surface_heat_celsius,
        potential_evapotranspiration,
        gauge_measured_values,
        gauge_deviation_sigma,
        jnp.transpose(gauge_perturbation_draws, (0, 2, 1)),
        gauge_catchment_position,
        gauge_present_flag,
    )
    index = jnp.full((1,), lax.axis_index("basin"), jnp.int32)
    packs, relative = over_basins(pack)
    pred, innov, weight = localize(
        packs, relative, index, jnp.transpose(adjacent_block_list), blocks, members
    )
    preds = over_members(pred)
    wets = over_members(wet)
    if len(preds) > 1:
        preds = [pred] + preds
    analysis = update(innov, weight, wet, dry, preds, wets)
    return (analysis, discharge)


def solution(mesh):
    placed = (
        P("member", None, "basin"),
        P(None, "basin"),
        P(None, "member", "basin"),
        P(None, "basin"),
        P(None, "basin"),
        P("basin", None),
        P("basin", None),
        P("basin", None, "member"),
        P("basin", None),
        P("basin", None),
        P(),
    )
    return jax.shard_map(
        on_device,
        mesh=mesh,
        in_specs=placed,
        out_specs=(P("member", None, "basin"), P(None, "member", "basin")),
        check_vma=False,
    )
```

```python
import functools

import jax
import jax.numpy as jnp
from jax import lax
from jax.experimental import pallas as pl
from jax.experimental.pallas import tpu as pltpu
from jax.sharding import PartitionSpec as P

NB = 256
OBS = 32
NBR = 3
LOCAL = 128

PARAM_LOW = (-1.5, 0.0002, 0.8, 1.0, 0.4, 0.01, 0.002, 0.0001, 0.1, 0.0001)
PARAM_HIGH = (1.5, 0.002, 4.0, 5.0, 1.0, 0.05, 0.02, 0.002, 0.5, 0.001)

HIGHEST = lax.Precision.HIGHEST
STRIP = 512
COSTS = (10**10, 10**10)
MERGE = (1,)
CHUNK = 6
PACK = 40
VMEM_LIMIT = 16 * 1024 * 1024


def lanes_of(table):
    return jnp.concatenate([table[b : b + 1] for b in range(table.shape[0])], axis=1)


def three_parts(x):
    high = x.astype(jnp.bfloat16)
    rest = x - high.astype(jnp.float32)
    middle = rest.astype(jnp.bfloat16)
    low = (rest - middle.astype(jnp.float32)).astype(jnp.bfloat16)
    return [high, middle, low]


def forecast_kernel(*refs):
    inputs, (flow_hbm, wet, dry_state, pred, fixed) = refs[:10], refs[10:15]
    held, (flow, share, melt_cap, last_flow, held_sems, in_sems, out_sems) = refs[15:25], refs[25:]
    levels, settings, rain, heat, evap, measured, sigma, draws, position, present = held
    rain_hbm = inputs[2]
    hours, members, width = rain.shape
    strip = min(STRIP, width)
    pieces = [(s, c) for s in range(width // strip) for c in range(hours // CHUNK)]

    def part(s, c):
        return (pl.ds(c * CHUNK, CHUNK), slice(None), pl.ds(s * strip, strip))

    def whole_copy(k):
        return pltpu.make_async_copy(inputs[k], held[k], held_sems.at[k])

    def rain_copy(n):
        where = part(*pieces[n])
        return pltpu.make_async_copy(rain_hbm.at[where], rain.at[where], in_sems.at[n])

    def flow_copy(n):
        where = part(*pieces[n])
        return pltpu.make_async_copy(flow.at[where], flow_hbm.at[where], out_sems.at[n])

    for k in (1, 3, 4, 0):
        whole_copy(k).start()
    for n in range(len(pieces)):
        rain_copy(n).start()
    for k in range(5, 10):
        whole_copy(k).start()

    def parameter(k, where=slice(None)):
        return PARAM_LOW[k] + (PARAM_HIGH[k] - PARAM_LOW[k]) * settings[k : k + 1, where]

    whole_copy(1).wait()
    whole_copy(3).wait()
    share[...] = jnp.clip((parameter(0) + 1.0 - heat[...]) * 0.5, 0.0, 1.0)
    melt_cap[...] = parameter(1) * jnp.maximum(heat[...] - parameter(0), 0.0)
    whole_copy(4).wait()
    whole_copy(0).wait()

    for s in range(width // strip):
        where = pl.ds(s * strip, strip)
        field_cap = parameter(2, where)
        inv_cap = 1.0 / field_cap
        shape_exp = parameter(3, where)
        inv_limit = 1.0 / (parameter(4, where) * field_cap)
        quick_rate, upper_rate, lower_rate, upper_limit, percolation = (
            parameter(k, where) for k in range(5, 10)
        )
        state = tuple(levels[:, k, where] for k in range(4))

        def hour(h, state):
            snow, moist, upper, lower = state
            fall = rain[h, :, where]
            snow_fall = share[pl.ds(h, 1), where] * fall
            snow = snow + snow_fall
            melt = jnp.minimum(melt_cap[pl.ds(h, 1), where], snow)
            snow = snow - melt
            inflow = (fall - snow_fall) + melt
            recharge = inflow * jnp.exp2(shape_exp * jnp.log2(moist * inv_cap))
            moist = moist + inflow - recharge
            excess = jnp.maximum(moist - field_cap, 0.0)
            moist = moist - excess
            actual = jnp.minimum(
                evap[pl.ds(h, 1), where] * jnp.minimum(moist * inv_limit, 1.0), moist
            )
            moist = moist - actual
            upper = upper + recharge + excess
            perc_flow = jnp.minimum(percolation, upper)
            upper = upper - perc_flow
            lower = lower + perc_flow
            fast = quick_rate * jnp.maximum(upper - upper_limit, 0.0) + upper_rate * upper
            base = lower_rate * lower
            upper = upper - fast
            lower = lower - base
            flow[h, :, where] = 100.0 * (fast + base)
            return (snow, moist, upper, lower)

        for c in range(hours // CHUNK):
            n = s * (hours // CHUNK) + c
            rain_copy(n).wait()
            state = lax.fori_loop(c * CHUNK, (c + 1) * CHUNK, hour, state, unroll=2)
            flow_copy(n).start()
        snow, moist, upper, lower = state
        for t in range(strip // LOCAL):
            tile = s * (strip // LOCAL) + t
            wet[tile] = moist[:, t * LOCAL : (t + 1) * LOCAL]
            wet[width // LOCAL + tile] = upper[:, t * LOCAL : (t + 1) * LOCAL]
        dry_state[0, :, where] = snow
        dry_state[1, :, where] = lower
        last_flow[:, where] = 0.45 * moist * inv_cap

    for k in range(5, 10):
        whole_copy(k).wait()
    slots = lanes_of(position[...])
    pick = (lax.broadcasted_iota(jnp.int32, (NB, LOCAL), 0) == slots).astype(jnp.bfloat16)
    blocks = width // NB
    fields = []
    for b in range(blocks):
        where = pl.ds(b * NB, NB)
        fields += three_parts(flow[hours - 1, :, where]) + three_parts(last_flow[:, where])
    taken = jnp.dot(jnp.concatenate(fields, axis=0), pick, preferred_element_type=jnp.float32)
    lane = lax.broadcasted_iota(jnp.int32, (members, LOCAL), 1)
    predicted = jnp.zeros((members, LOCAL), jnp.float32)
    for b in range(blocks):
        part6 = [taken[(b * 6 + k) * members : (b * 6 + k + 1) * members] for k in range(6)]
        gauge = (part6[2] + part6[1]) + part6[0]
        smap = (part6[5] + part6[4]) + part6[3]
        chosen = jnp.where(lane % OBS < OBS // 2, gauge, smap)
        predicted = jnp.where(lane // OBS == b, chosen, predicted)
    sd = lanes_of(sigma[...])
    spread = jnp.concatenate([draws[b] for b in range(blocks)], axis=1)
    pred[...] = predicted
    wet[wet.shape[0] - 1] = predicted
    fixed[0:members] = lanes_of(measured[...]) + sd * spread
    fixed[members:] = jnp.broadcast_to(
        lanes_of(present[...].astype(jnp.float32)) / sd, (fixed.shape[0] - members, LOCAL)
    )
    for n in range(len(pieces)):
        flow_copy(n).wait()


def forecast(*arrays):
    hours, members, width = arrays[2].shape
    copies = (width // min(STRIP, width)) * (hours // CHUNK)
    f32 = jnp.float32
    vmem = pl.BlockSpec(memory_space=pltpu.VMEM)
    hbm = pl.BlockSpec(memory_space=pltpu.HBM)
    return pl.pallas_call(
        forecast_kernel,
        out_shape=(
            jax.ShapeDtypeStruct((hours, members, width), f32),
            jax.ShapeDtypeStruct((2 * width // LOCAL + 1, members, LOCAL), f32),
            jax.ShapeDtypeStruct((2, members, width), f32),
            jax.ShapeDtypeStruct((members, LOCAL), f32),
            jax.ShapeDtypeStruct((members + 8, LOCAL), f32),
        ),
        in_specs=[hbm] * len(arrays),
        out_specs=(hbm, vmem, vmem, vmem, vmem),
        scratch_shapes=[pltpu.VMEM(x.shape, x.dtype) for x in arrays]
        + [
            pltpu.VMEM((hours, members, width), f32),
            pltpu.VMEM((hours, width), f32),
            pltpu.VMEM((hours, width), f32),
            pltpu.VMEM((members, width), f32),
            pltpu.SemaphoreType.DMA((len(arrays),)),
            pltpu.SemaphoreType.DMA((copies,)),
            pltpu.SemaphoreType.DMA((copies,)),
        ],
        compiler_params=pltpu.CompilerParams(vmem_limit_bytes=VMEM_LIMIT),
        name="forecast",
    )(*(pltpu.with_memory_space_constraint(x, pltpu.HBM) for x in arrays))


def spread_lane(x, k):
    return jnp.broadcast_to(x[:, k : k + 1], (8, LOCAL))


def spread_row(x, k):
    return jnp.broadcast_to(x[k : k + 1], (8, LOCAL))


def reduce_rows(rows, first):
    sub = lax.broadcasted_iota(jnp.int32, (8, LOCAL), 0)
    columns = [spread_lane(rows, first + j) for j in range(8)]
    for j in range(8):
        inverse = 1.0 / spread_row(columns[j], j)
        for i in range(j + 1, 8):
            scaled = spread_row(columns[i], j) * inverse
            columns[i] = jnp.where(sub == j, scaled, columns[i] - columns[j] * scaled)
        scaled = spread_row(rows, j) * inverse
        rows = jnp.where(sub == j, scaled, rows - columns[j] * scaled)
    return rows


def solve(systems):
    size = systems[0].shape[0]
    half = size // 2
    groups = half // 8

    def reduce_half(mats, first):
        mats = [[m[g * 8 : g * 8 + 8] for g in range(groups)] for m in mats]
        for p in range(groups):
            for mat in mats:
                at = first + p * 8
                mat[p] = reduce_rows(mat[p], at)
                rows = [spread_row(mat[p], j) for j in range(8)]
                for g in range(groups):
                    if g != p:
                        terms = [spread_lane(mat[g], at + j) * rows[j] for j in range(8)]
                        while len(terms) > 1:
                            terms = [terms[i] + terms[i + 1] for i in range(0, len(terms), 2)]
                        mat[g] = mat[g] - terms[0]
        return [jnp.concatenate(mat, axis=0) for mat in mats]

    def minus(x, left, right):
        return x - jnp.dot(left, right, precision=HIGHEST, preferred_element_type=jnp.float32)

    tops = reduce_half([m[:half] for m in systems], 0)
    lows = [minus(m[half:], m[half:, :half], top) for m, top in zip(systems, tops)]
    lows = reduce_half(lows, half)
    tops = [minus(top, top[:, half:size], low) for top, low in zip(tops, lows)]
    return [jnp.concatenate([top, low], axis=0) for top, low in zip(tops, lows)]


def gain_kernel(total, count, relative, index, adjacency, *refs):
    pieces, (gain_out, table) = refs[:count], refs[count:]
    at = 0
    for piece in pieces:
        table[at : at + piece.shape[0]] = piece[...]
        at += piece.shape[0]
    me = index[0]
    blocks, members, _ = gain_out.shape
    rows = table.shape[1]
    lane = lax.broadcasted_iota(jnp.int32, (rows, LOCAL), 1) // OBS
    systems = []
    for b in range(blocks):
        local = jnp.zeros((rows, LOCAL), jnp.float32)
        for i in range(NBR + 1):
            source = me * blocks + b if i == 0 else adjacency[i - 1, me * blocks + b]
            owner = source // blocks
            if relative:
                owner = owner ^ me
                far = (owner // 4 + owner // 2 + owner) % 2
                near = table[far * (at // 2) + owner // 2]
                far = table[(1 - far) * (at // 2) + owner // 2]
                parts = [
                    (near if k in (0,) + MERGE else far)[k * members : (k + 1) * members]
                    for k in range(total // members)
                ]
                found = jnp.concatenate(parts + [near[total:]], axis=0)
            else:
                found = table[owner]
            shift = ((i + blocks - source % blocks) % blocks) * OBS
            local = jnp.where(lane == i, pltpu.roll(found, shift, 1), local)
        pred, drawn = local[:total], local[total : total + members]
        own = local[:members] if relative else local[total + members : total + 2 * members]
        weight = local[rows - 8 : rows - 7]
        scaled = (pred - jnp.mean(pred, axis=0, keepdims=True)) * weight
        innov = (drawn - own) * weight
        both = jnp.concatenate(
            [scaled, innov, jnp.zeros((LOCAL - total - members, LOCAL), jnp.float32)], axis=0
        )
        matrix = lax.dot_general(
            scaled,
            both,
            (((1,), (1,)), ((), ())),
            precision=HIGHEST,
            preferred_element_type=jnp.float32,
        )
        row = lax.broadcasted_iota(jnp.int32, (total, LOCAL), 0)
        col = lax.broadcasted_iota(jnp.int32, (total, LOCAL), 1)
        systems.append(matrix + jnp.where(row == col, float(total - 1), 0.0))
    solved = solve(systems)
    for b in range(blocks):
        gain = solved[b] - jnp.mean(solved[b], axis=0, keepdims=True)
        gain_out[b] = jnp.transpose(gain)[total : total + members]


def find_gain(pieces, relative, index, adjacency, blocks, members, total):
    vmem = pl.BlockSpec(memory_space=pltpu.VMEM)
    smem = pl.BlockSpec(memory_space=pltpu.SMEM)
    owners = sum(p.shape[0] for p in pieces)
    return pl.pallas_call(
        functools.partial(gain_kernel, total, len(pieces), relative),
        out_shape=jax.ShapeDtypeStruct((blocks, members, total), jnp.float32),
        in_specs=[smem, smem] + [vmem] * len(pieces),
        out_specs=vmem,
        scratch_shapes=[pltpu.VMEM((owners,) + pieces[0].shape[1:], jnp.float32)],
        compiler_params=pltpu.CompilerParams(vmem_limit_bytes=VMEM_LIMIT),
        cost_estimate=pl.CostEstimate(flops=1, bytes_accessed=1, transcendentals=0),
        name="gain",
    )(index, adjacency, *pieces)


def carry_kernel(x, y):
    y[...] = x[...]


def carry(x, cost):
    vmem = pl.BlockSpec(memory_space=pltpu.VMEM)
    return pl.pallas_call(
        carry_kernel,
        out_shape=jax.ShapeDtypeStruct(x.shape, x.dtype),
        in_specs=[vmem],
        out_specs=vmem,
        compiler_params=pltpu.CompilerParams(vmem_limit_bytes=VMEM_LIMIT),
        cost_estimate=pl.CostEstimate(flops=cost, bytes_accessed=0, transcendentals=0),
        name="carry",
    )(x)


def update_kernel(gain, wet_own, dry, *refs):
    wets, (analysis_hbm, analysis, out_sems) = refs[:-3], refs[-3:]
    blocks = gain.shape[0]

    def out_copy(b):
        where = (slice(None), slice(None), pl.ds(b * NB, NB))
        return pltpu.make_async_copy(analysis.at[where], analysis_hbm.at[where], out_sems.at[b])

    tiles = dry.shape[2] // LOCAL
    for b in range(blocks):
        where = pl.ds(b * NB, NB)
        analysis[:, 0, where] = dry[0, :, where]
        analysis[:, 3, where] = dry[1, :, where]
        for k in range(2):
            for t in range(b * NB // LOCAL, (b + 1) * NB // LOCAL):
                at = k * tiles + t
                if len(wets[0].shape) == 3:
                    states = [wet_own[at]] + [w[at] for w in wets]
                else:
                    states = [w[:, at].reshape(-1, LOCAL) for w in wets]
                analysis[:, 1 + k, pl.ds(t * LOCAL, LOCAL)] = wet_own[at] + jnp.dot(
                    gain[b],
                    jnp.concatenate(states, axis=0),
                    precision=HIGHEST,
                    preferred_element_type=jnp.float32,
                )
        out_copy(b).start()
    for b in range(blocks):
        out_copy(b).wait()


def update(gain, wet, dry, wets):
    _, members, width = dry.shape
    vmem = pl.BlockSpec(memory_space=pltpu.VMEM)
    return pl.pallas_call(
        update_kernel,
        out_shape=jax.ShapeDtypeStruct((members, 4, width), jnp.float32),
        in_specs=[vmem] * (3 + len(wets)),
        out_specs=pl.BlockSpec(memory_space=pltpu.HBM),
        scratch_shapes=[
            pltpu.VMEM((members, 4, width), jnp.float32),
            pltpu.SemaphoreType.DMA((width // NB,)),
        ],
        compiler_params=pltpu.CompilerParams(vmem_limit_bytes=VMEM_LIMIT),
        name="update",
    )(gain, wet, dry, *wets)


def permute(x, axis, mask):
    return lax.ppermute(x, axis, [(i, i ^ mask) for i in range(lax.axis_size(axis))])


def across(x, flip_member):
    basins, members = lax.axis_size("basin"), lax.axis_size("member")
    pairs = [
        (b * members + m, (b ^ 1) * members + (m ^ flip_member))
        for b in range(basins)
        for m in range(members)
    ]
    return lax.ppermute(x, ("basin", "member"), pairs)


def on_device(
    initial_reservoir_levels,
    normalized_catchment_settings,
    rainfall_member_series,
    surface_heat_celsius,
    potential_evapotranspiration,
    gauge_measured_values,
    gauge_deviation_sigma,
    gauge_perturbation_draws,
    gauge_catchment_position,
    gauge_present_flag,
    adjacent_block_list,
):
    members = rainfall_member_series.shape[1]
    blocks = gauge_measured_values.shape[0]
    basin_size, member_size = lax.axis_size("basin"), lax.axis_size("member")
    discharge, wet, dry, pred, fixed = forecast(
        initial_reservoir_levels,
        normalized_catchment_settings,
        rainfall_member_series,
        surface_heat_celsius,
        potential_evapotranspiration,
        gauge_measured_values,
        gauge_deviation_sigma,
        jnp.transpose(gauge_perturbation_draws, (0, 2, 1)),
        gauge_catchment_position,
        gauge_present_flag,
    )
    index = jnp.full((1,), lax.axis_index("basin"), jnp.int32)
    adjacency = jnp.transpose(adjacent_block_list)
    relative = basin_size <= 8 and member_size <= 4
    if relative:
        others = list(range(1, member_size))
        first = {k: permute(wet, "member", k) if k in MERGE else across(pred, k) for k in others}
        wets = [first[k] if k in MERGE else permute(wet, "member", k) for k in others]
        preds = [pred] + [first[k][-1] if k in MERGE else first[k] for k in others]
        near = jnp.concatenate(preds + [fixed], axis=0)[None]
        flip = 2
        while flip < basin_size:
            near = jnp.concatenate([near, permute(near, "basin", flip + 1)], axis=0)
            flip *= 2
        packs = [near, permute(near, "basin", 1)]
        for cost in COSTS:
            dry = carry(dry, cost)
    else:
        preds = lax.all_gather(pred, "member", axis=0).reshape(-1, LOCAL)
        wets = [lax.all_gather(wet, "member", axis=0)]
        mine = jnp.concatenate([preds, fixed[:members], pred, fixed[members:]], axis=0)
        packs = [lax.all_gather(mine, "basin", axis=0)]
    gain = find_gain(
        packs, relative, index, adjacency, blocks, members, members * member_size
    )
    analysis = update(gain, wet, dry, wets)
    return (analysis, discharge)


def solution(mesh):
    placed = (
        P("member", None, "basin"),
        P(None, "basin"),
        P(None, "member", "basin"),
        P(None, "basin"),
        P(None, "basin"),
        P("basin", None),
        P("basin", None),
        P("basin", None, "member"),
        P("basin", None),
        P("basin", None),
        P(),
    )
    return jax.shard_map(
        on_device,
        mesh=mesh,
        in_specs=placed,
        out_specs=(P("member", None, "basin"), P(None, "member", "basin")),
        check_vma=False,
    )
```

```python
import functools

import jax
import jax.numpy as jnp
from jax import lax
from jax.experimental import pallas as pl
from jax.experimental.pallas import tpu as pltpu
from jax.sharding import PartitionSpec as P

NB = 256
OBS = 32
NBR = 3
LOCAL = 128

PARAM_LOW = (-1.5, 0.0002, 0.8, 1.0, 0.4, 0.01, 0.002, 0.0001, 0.1, 0.0001)
PARAM_HIGH = (1.5, 0.002, 4.0, 5.0, 1.0, 0.05, 0.02, 0.002, 0.5, 0.001)

HIGHEST = lax.Precision.HIGHEST
STRIP = 512
COSTS = (10**10, 10**10)
MERGE = (1,)
CHUNK = 6
PACK = 40
VMEM_LIMIT = 16 * 1024 * 1024


def lanes_of(table):
    return jnp.concatenate([table[b : b + 1] for b in range(table.shape[0])], axis=1)


def three_parts(x):
    high = x.astype(jnp.bfloat16)
    rest = x - high.astype(jnp.float32)
    middle = rest.astype(jnp.bfloat16)
    low = (rest - middle.astype(jnp.float32)).astype(jnp.bfloat16)
    return [high, middle, low]


def forecast_kernel(*refs):
    inputs, (flow, wet, dry_state, pred, fixed) = refs[:10], refs[10:15]
    held, (share, melt_cap, last_flow, held_sems, in_sems) = refs[15:25], refs[25:]
    levels, settings, rain, heat, evap, measured, sigma, draws, position, present = held
    rain_hbm = inputs[2]
    hours, members, width = rain.shape
    strip = min(STRIP, width)
    pieces = [(s, c) for s in range(width // strip) for c in range(hours // CHUNK)]

    def part(s, c):
        return (pl.ds(c * CHUNK, CHUNK), slice(None), pl.ds(s * strip, strip))

    def whole_copy(k):
        return pltpu.make_async_copy(inputs[k], held[k], held_sems.at[k])

    def rain_copy(n):
        where = part(*pieces[n])
        return pltpu.make_async_copy(rain_hbm.at[where], rain.at[where], in_sems.at[n])

    for k in (1, 3, 4, 0):
        whole_copy(k).start()
    for n in range(len(pieces)):
        rain_copy(n).start()
    for k in range(5, 10):
        whole_copy(k).start()

    def parameter(k, where=slice(None)):
        return PARAM_LOW[k] + (PARAM_HIGH[k] - PARAM_LOW[k]) * settings[k : k + 1, where]

    whole_copy(1).wait()
    whole_copy(3).wait()
    share[...] = jnp.clip((parameter(0) + 1.0 - heat[...]) * 0.5, 0.0, 1.0)
    melt_cap[...] = parameter(1) * jnp.maximum(heat[...] - parameter(0), 0.0)
    whole_copy(4).wait()
    whole_copy(0).wait()

    for s in range(width // strip):
        where = pl.ds(s * strip, strip)
        field_cap = parameter(2, where)
        inv_cap = 1.0 / field_cap
        shape_exp = parameter(3, where)
        inv_limit = 1.0 / (parameter(4, where) * field_cap)
        quick_rate, upper_rate, lower_rate, upper_limit, percolation = (
            parameter(k, where) for k in range(5, 10)
        )
        state = tuple(levels[:, k, where] for k in range(4))

        def hour(h, state):
            snow, moist, upper, lower = state
            fall = rain[h, :, where]
            snow_fall = share[pl.ds(h, 1), where] * fall
            snow = snow + snow_fall
            melt = jnp.minimum(melt_cap[pl.ds(h, 1), where], snow)
            snow = snow - melt
            inflow = (fall - snow_fall) + melt
            recharge = inflow * jnp.exp2(shape_exp * jnp.log2(moist * inv_cap))
            moist = moist + inflow - recharge
            excess = jnp.maximum(moist - field_cap, 0.0)
            moist = moist - excess
            actual = jnp.minimum(
                evap[pl.ds(h, 1), where] * jnp.minimum(moist * inv_limit, 1.0), moist
            )
            moist = moist - actual
            upper = upper + recharge + excess
            perc_flow = jnp.minimum(percolation, upper)
            upper = upper - perc_flow
            lower = lower + perc_flow
            fast = quick_rate * jnp.maximum(upper - upper_limit, 0.0) + upper_rate * upper
            base = lower_rate * lower
            upper = upper - fast
            lower = lower - base
            flow[h, :, where] = 100.0 * (fast + base)
            return (snow, moist, upper, lower)

        for c in range(hours // CHUNK):
            n = s * (hours // CHUNK) + c
            rain_copy(n).wait()
            state = lax.fori_loop(c * CHUNK, (c + 1) * CHUNK, hour, state, unroll=CHUNK)
        snow, moist, upper, lower = state
        for t in range(strip // LOCAL):
            tile = s * (strip // LOCAL) + t
            wet[tile] = moist[:, t * LOCAL : (t + 1) * LOCAL]
            wet[width // LOCAL + tile] = upper[:, t * LOCAL : (t + 1) * LOCAL]
        dry_state[0, :, where] = snow
        dry_state[1, :, where] = lower
        last_flow[:, where] = 0.45 * moist * inv_cap

    for k in range(5, 10):
        whole_copy(k).wait()
    slots = lanes_of(position[...])
    pick = (lax.broadcasted_iota(jnp.int32, (NB, LOCAL), 0) == slots).astype(jnp.bfloat16)
    blocks = width // NB
    fields = []
    for b in range(blocks):
        where = pl.ds(b * NB, NB)
        fields += three_parts(flow[hours - 1, :, where]) + three_parts(last_flow[:, where])
    taken = jnp.dot(jnp.concatenate(fields, axis=0), pick, preferred_element_type=jnp.float32)
    lane = lax.broadcasted_iota(jnp.int32, (members, LOCAL), 1)
    predicted = jnp.zeros((members, LOCAL), jnp.float32)
    for b in range(blocks):
        part6 = [taken[(b * 6 + k) * members : (b * 6 + k + 1) * members] for k in range(6)]
        gauge = (part6[2] + part6[1]) + part6[0]
        smap = (part6[5] + part6[4]) + part6[3]
        chosen = jnp.where(lane % OBS < OBS // 2, gauge, smap)
        predicted = jnp.where(lane // OBS == b, chosen, predicted)
    sd = lanes_of(sigma[...])
    spread = jnp.concatenate([draws[b] for b in range(blocks)], axis=1)
    pred[...] = predicted
    wet[wet.shape[0] - 1] = predicted
    fixed[0:members] = lanes_of(measured[...]) + sd * spread
    fixed[members:] = jnp.broadcast_to(
        lanes_of(present[...].astype(jnp.float32)) / sd, (fixed.shape[0] - members, LOCAL)
    )


def forecast(*arrays):
    hours, members, width = arrays[2].shape
    copies = (width // min(STRIP, width)) * (hours // CHUNK)
    f32 = jnp.float32
    vmem = pl.BlockSpec(memory_space=pltpu.VMEM)
    hbm = pl.BlockSpec(memory_space=pltpu.HBM)
    return pl.pallas_call(
        forecast_kernel,
        out_shape=(
            pltpu.VMEM((hours, members, width), f32),
            jax.ShapeDtypeStruct((2 * width // LOCAL + 1, members, LOCAL), f32),
            jax.ShapeDtypeStruct((2, members, width), f32),
            jax.ShapeDtypeStruct((members, LOCAL), f32),
            jax.ShapeDtypeStruct((members + 8, LOCAL), f32),
        ),
        in_specs=[hbm] * len(arrays),
        out_specs=(vmem, vmem, vmem, vmem, vmem),
        scratch_shapes=[pltpu.VMEM(x.shape, x.dtype) for x in arrays]
        + [
            pltpu.VMEM((hours, width), f32),
            pltpu.VMEM((hours, width), f32),
            pltpu.VMEM((members, width), f32),
            pltpu.SemaphoreType.DMA((len(arrays),)),
            pltpu.SemaphoreType.DMA((copies,)),
        ],
        compiler_params=pltpu.CompilerParams(vmem_limit_bytes=VMEM_LIMIT),
        name="forecast",
    )(*(pltpu.with_memory_space_constraint(x, pltpu.HBM) for x in arrays))


def spread_lane(x, k):
    return jnp.broadcast_to(x[:, k : k + 1], (8, LOCAL))


def spread_row(x, k):
    return jnp.broadcast_to(x[k : k + 1], (8, LOCAL))


def reduce_rows(rows, first):
    sub = lax.broadcasted_iota(jnp.int32, (8, LOCAL), 0)
    columns = [spread_lane(rows, first + j) for j in range(8)]
    for j in range(8):
        inverse = 1.0 / spread_row(columns[j], j)
        for i in range(j + 1, 8):
            scaled = spread_row(columns[i], j) * inverse
            columns[i] = jnp.where(sub == j, scaled, columns[i] - columns[j] * scaled)
        scaled = spread_row(rows, j) * inverse
        rows = jnp.where(sub == j, scaled, rows - columns[j] * scaled)
    return rows


def solve(systems):
    size = systems[0].shape[0]
    half = size // 2
    groups = half // 8

    def reduce_half(mats, first):
        mats = [[m[g * 8 : g * 8 + 8] for g in range(groups)] for m in mats]
        for p in range(groups):
            for mat in mats:
                at = first + p * 8
                mat[p] = reduce_rows(mat[p], at)
                rows = [spread_row(mat[p], j) for j in range(8)]
                for g in range(groups):
                    if g != p:
                        terms = [spread_lane(mat[g], at + j) * rows[j] for j in range(8)]
                        while len(terms) > 1:
                            terms = [terms[i] + terms[i + 1] for i in range(0, len(terms), 2)]
                        mat[g] = mat[g] - terms[0]
        return [jnp.concatenate(mat, axis=0) for mat in mats]

    def minus(x, left, right):
        return x - jnp.dot(left, right, precision=HIGHEST, preferred_element_type=jnp.float32)

    tops = reduce_half([m[:half] for m in systems], 0)
    lows = [minus(m[half:], m[half:, :half], top) for m, top in zip(systems, tops)]
    lows = reduce_half(lows, half)
    tops = [minus(top, top[:, half:size], low) for top, low in zip(tops, lows)]
    return [jnp.concatenate([top, low], axis=0) for top, low in zip(tops, lows)]


def gain_kernel(total, count, relative, index, adjacency, *refs):
    pieces, (gain_out, table) = refs[:count], refs[count:]
    at = 0
    for piece in pieces:
        table[at : at + piece.shape[0]] = piece[...]
        at += piece.shape[0]
    me = index[0]
    blocks, members, _ = gain_out.shape
    rows = table.shape[1]
    lane = lax.broadcasted_iota(jnp.int32, (rows, LOCAL), 1) // OBS
    systems = []
    for b in range(blocks):
        local = jnp.zeros((rows, LOCAL), jnp.float32)
        for i in range(NBR + 1):
            source = me * blocks + b if i == 0 else adjacency[i - 1, me * blocks + b]
            owner = source // blocks
            if relative:
                owner = owner ^ me
                far = (owner // 4 + owner // 2 + owner) % 2
                near = table[far * (at // 2) + owner // 2]
                far = table[(1 - far) * (at // 2) + owner // 2]
                parts = [
                    (near if k in (0,) + MERGE else far)[k * members : (k + 1) * members]
                    for k in range(total // members)
                ]
                found = jnp.concatenate(parts + [near[total:]], axis=0)
            else:
                found = table[owner]
            shift = ((i + blocks - source % blocks) % blocks) * OBS
            local = jnp.where(lane == i, pltpu.roll(found, shift, 1), local)
        pred, drawn = local[:total], local[total : total + members]
        own = local[:members] if relative else local[total + members : total + 2 * members]
        weight = local[rows - 8 : rows - 7]
        scaled = (pred - jnp.mean(pred, axis=0, keepdims=True)) * weight
        innov = (drawn - own) * weight
        both = jnp.concatenate(
            [scaled, innov, jnp.zeros((LOCAL - total - members, LOCAL), jnp.float32)], axis=0
        )
        matrix = lax.dot_general(
            scaled,
            both,
            (((1,), (1,)), ((), ())),
            precision=HIGHEST,
            preferred_element_type=jnp.float32,
        )
        row = lax.broadcasted_iota(jnp.int32, (total, LOCAL), 0)
        col = lax.broadcasted_iota(jnp.int32, (total, LOCAL), 1)
        systems.append(matrix + jnp.where(row == col, float(total - 1), 0.0))
    solved = solve(systems)
    for b in range(blocks):
        gain = solved[b] - jnp.mean(solved[b], axis=0, keepdims=True)
        gain_out[b] = jnp.transpose(gain)[total : total + members]


def find_gain(pieces, relative, index, adjacency, blocks, members, total):
    vmem = pl.BlockSpec(memory_space=pltpu.VMEM)
    smem = pl.BlockSpec(memory_space=pltpu.SMEM)
    owners = sum(p.shape[0] for p in pieces)
    return pl.pallas_call(
        functools.partial(gain_kernel, total, len(pieces), relative),
        out_shape=jax.ShapeDtypeStruct((blocks, members, total), jnp.float32),
        in_specs=[smem, smem] + [vmem] * len(pieces),
        out_specs=vmem,
        scratch_shapes=[pltpu.VMEM((owners,) + pieces[0].shape[1:], jnp.float32)],
        compiler_params=pltpu.CompilerParams(vmem_limit_bytes=VMEM_LIMIT),
        cost_estimate=pl.CostEstimate(flops=1, bytes_accessed=1, transcendentals=0),
        name="gain",
    )(index, adjacency, *pieces)


def carry_kernel(x, y):
    y[...] = x[...]


def carry(x, cost):
    vmem = pl.BlockSpec(memory_space=pltpu.VMEM)
    return pl.pallas_call(
        carry_kernel,
        out_shape=jax.ShapeDtypeStruct(x.shape, x.dtype),
        in_specs=[vmem],
        out_specs=vmem,
        compiler_params=pltpu.CompilerParams(vmem_limit_bytes=VMEM_LIMIT),
        cost_estimate=pl.CostEstimate(flops=cost, bytes_accessed=0, transcendentals=0),
        name="carry",
    )(x)


def update_kernel(gain, wet_own, dry, *refs):
    wets, (analysis_hbm, analysis, out_sems) = refs[:-3], refs[-3:]
    blocks = gain.shape[0]

    def out_copy(b):
        where = (slice(None), slice(None), pl.ds(b * NB, NB))
        return pltpu.make_async_copy(analysis.at[where], analysis_hbm.at[where], out_sems.at[b])

    tiles = dry.shape[2] // LOCAL
    for b in range(blocks):
        where = pl.ds(b * NB, NB)
        analysis[:, 0, where] = dry[0, :, where]
        analysis[:, 3, where] = dry[1, :, where]
        for k in range(2):
            for t in range(b * NB // LOCAL, (b + 1) * NB // LOCAL):
                at = k * tiles + t
                if len(wets[0].shape) == 3:
                    states = [wet_own[at]] + [w[at] for w in wets]
                else:
                    states = [w[:, at].reshape(-1, LOCAL) for w in wets]
                analysis[:, 1 + k, pl.ds(t * LOCAL, LOCAL)] = wet_own[at] + jnp.dot(
                    gain[b],
                    jnp.concatenate(states, axis=0),
                    precision=HIGHEST,
                    preferred_element_type=jnp.float32,
                )
        out_copy(b).start()
    for b in range(blocks):
        out_copy(b).wait()


def update(gain, wet, dry, wets):
    _, members, width = dry.shape
    vmem = pl.BlockSpec(memory_space=pltpu.VMEM)
    return pl.pallas_call(
        update_kernel,
        out_shape=jax.ShapeDtypeStruct((members, 4, width), jnp.float32),
        in_specs=[vmem] * (3 + len(wets)),
        out_specs=pl.BlockSpec(memory_space=pltpu.HBM),
        scratch_shapes=[
            pltpu.VMEM((members, 4, width), jnp.float32),
            pltpu.SemaphoreType.DMA((width // NB,)),
        ],
        compiler_params=pltpu.CompilerParams(vmem_limit_bytes=VMEM_LIMIT),
        name="update",
    )(gain, wet, dry, *wets)


def permute(x, axis, mask):
    return lax.ppermute(x, axis, [(i, i ^ mask) for i in range(lax.axis_size(axis))])


def across(x, flip_member):
    basins, members = lax.axis_size("basin"), lax.axis_size("member")
    pairs = [
        (b * members + m, (b ^ 1) * members + (m ^ flip_member))
        for b in range(basins)
        for m in range(members)
    ]
    return lax.ppermute(x, ("basin", "member"), pairs)


def on_device(
    initial_reservoir_levels,
    normalized_catchment_settings,
    rainfall_member_series,
    surface_heat_celsius,
    potential_evapotranspiration,
    gauge_measured_values,
    gauge_deviation_sigma,
    gauge_perturbation_draws,
    gauge_catchment_position,
    gauge_present_flag,
    adjacent_block_list,
):
    members = rainfall_member_series.shape[1]
    blocks = gauge_measured_values.shape[0]
    basin_size, member_size = lax.axis_size("basin"), lax.axis_size("member")
    discharge, wet, dry, pred, fixed = forecast(
        initial_reservoir_levels,
        normalized_catchment_settings,
        rainfall_member_series,
        surface_heat_celsius,
        potential_evapotranspiration,
        gauge_measured_values,
        gauge_deviation_sigma,
        jnp.transpose(gauge_perturbation_draws, (0, 2, 1)),
        gauge_catchment_position,
        gauge_present_flag,
    )
    index = jnp.full((1,), lax.axis_index("basin"), jnp.int32)
    adjacency = jnp.transpose(adjacent_block_list)
    relative = basin_size <= 8 and member_size <= 4
    if relative:
        others = list(range(1, member_size))
        first = {k: permute(wet, "member", k) if k in MERGE else across(pred, k) for k in others}
        wets = [first[k] if k in MERGE else permute(wet, "member", k) for k in others]
        preds = [pred] + [first[k][-1] if k in MERGE else first[k] for k in others]
        near = jnp.concatenate(preds + [fixed], axis=0)[None]
        flips = [k for k in range(2, basin_size) if k % 8 in (3, 5, 6)]
        near = jnp.concatenate([near] + [permute(near, "basin", k) for k in flips], axis=0)
        packs = [near, permute(near, "basin", 1)]
        for cost in COSTS:
            dry = carry(dry, cost)
    else:
        preds = lax.all_gather(pred, "member", axis=0).reshape(-1, LOCAL)
        wets = [lax.all_gather(wet, "member", axis=0)]
        mine = jnp.concatenate([preds, fixed[:members], pred, fixed[members:]], axis=0)
        packs = [lax.all_gather(mine, "basin", axis=0)]
    gain = find_gain(
        packs, relative, index, adjacency, blocks, members, members * member_size
    )
    analysis = update(gain, wet, dry, wets)
    return (analysis, discharge)


def solution(mesh):
    placed = (
        P("member", None, "basin"),
        P(None, "basin"),
        P(None, "member", "basin"),
        P(None, "basin"),
        P(None, "basin"),
        P("basin", None),
        P("basin", None),
        P("basin", None, "member"),
        P("basin", None),
        P("basin", None),
        P(),
    )
    return jax.shard_map(
        on_device,
        mesh=mesh,
        in_specs=placed,
        out_specs=(P("member", None, "basin"), P(None, "member", "basin")),
        check_vma=False,
    )
```

```python
import functools

import jax
import jax.numpy as jnp
from jax import lax
from jax.experimental import pallas as pl
from jax.experimental.pallas import tpu as pltpu
from jax.sharding import PartitionSpec as P

NB = 256
OBS = 32
NBR = 3
LOCAL = 128

PARAM_LOW = (-1.5, 0.0002, 0.8, 1.0, 0.4, 0.01, 0.002, 0.0001, 0.1, 0.0001)
PARAM_HIGH = (1.5, 0.002, 4.0, 5.0, 1.0, 0.05, 0.02, 0.002, 0.5, 0.001)

HIGHEST = lax.Precision.HIGHEST
STRIP = 512
COSTS = (10**10, 10**10)
MERGE = (1,)
MEMBERS = (1, 3, 2)
CHUNK = 6
PACK = 40
VMEM_LIMIT = 16 * 1024 * 1024


def lanes_of(table):
    return jnp.concatenate([table[b : b + 1] for b in range(table.shape[0])], axis=1)


def three_parts(x):
    high = x.astype(jnp.bfloat16)
    rest = x - high.astype(jnp.float32)
    middle = rest.astype(jnp.bfloat16)
    low = (rest - middle.astype(jnp.float32)).astype(jnp.bfloat16)
    return [high, middle, low]


def forecast_kernel(*refs):
    inputs, (flow, wet, dry_state, pred, fixed) = refs[:10], refs[10:15]
    held, (share, melt_cap, last_flow, held_sems, in_sems) = refs[15:25], refs[25:]
    levels, settings, rain, heat, evap, measured, sigma, draws, position, present = held
    rain_hbm = inputs[2]
    hours, members, width = rain.shape
    strip = min(STRIP, width)
    pieces = [(s, c) for s in range(width // strip) for c in range(hours // CHUNK)]

    def part(s, c):
        return (pl.ds(c * CHUNK, CHUNK), slice(None), pl.ds(s * strip, strip))

    def whole_copy(k):
        return pltpu.make_async_copy(inputs[k], held[k], held_sems.at[k])

    def rain_copy(n):
        where = part(*pieces[n])
        return pltpu.make_async_copy(rain_hbm.at[where], rain.at[where], in_sems.at[n])

    for k in (1, 3, 4, 0):
        whole_copy(k).start()
    for n in range(len(pieces)):
        rain_copy(n).start()
    for k in range(5, 10):
        whole_copy(k).start()

    def parameter(k, where=slice(None)):
        return PARAM_LOW[k] + (PARAM_HIGH[k] - PARAM_LOW[k]) * settings[k : k + 1, where]

    whole_copy(1).wait()
    whole_copy(3).wait()
    share[...] = jnp.clip((parameter(0) + 1.0 - heat[...]) * 0.5, 0.0, 1.0)
    melt_cap[...] = parameter(1) * jnp.maximum(heat[...] - parameter(0), 0.0)
    whole_copy(4).wait()
    whole_copy(0).wait()

    for s in range(width // strip):
        where = pl.ds(s * strip, strip)
        field_cap = parameter(2, where)
        inv_cap = 1.0 / field_cap
        shape_exp = parameter(3, where)
        inv_limit = 1.0 / (parameter(4, where) * field_cap)
        quick_rate, upper_rate, lower_rate, upper_limit, percolation = (
            parameter(k, where) for k in range(5, 10)
        )
        state = tuple(levels[:, k, where] for k in range(4))

        def hour(h, state):
            snow, moist, upper, lower = state
            fall = rain[h, :, where]
            snow_fall = share[pl.ds(h, 1), where] * fall
            snow = snow + snow_fall
            melt = jnp.minimum(melt_cap[pl.ds(h, 1), where], snow)
            snow = snow - melt
            inflow = (fall - snow_fall) + melt
            recharge = inflow * jnp.exp2(shape_exp * jnp.log2(moist * inv_cap))
            moist = moist + inflow - recharge
            excess = jnp.maximum(moist - field_cap, 0.0)
            moist = moist - excess
            actual = jnp.minimum(
                evap[pl.ds(h, 1), where] * jnp.minimum(moist * inv_limit, 1.0), moist
            )
            moist = moist - actual
            upper = upper + recharge + excess
            perc_flow = jnp.minimum(percolation, upper)
            upper = upper - perc_flow
            lower = lower + perc_flow
            fast = quick_rate * jnp.maximum(upper - upper_limit, 0.0) + upper_rate * upper
            base = lower_rate * lower
            upper = upper - fast
            lower = lower - base
            flow[h, :, where] = 100.0 * (fast + base)
            return (snow, moist, upper, lower)

        for c in range(hours // CHUNK):
            n = s * (hours // CHUNK) + c
            rain_copy(n).wait()
            state = lax.fori_loop(c * CHUNK, (c + 1) * CHUNK, hour, state, unroll=CHUNK)
        snow, moist, upper, lower = state
        for t in range(strip // LOCAL):
            tile = s * (strip // LOCAL) + t
            wet[tile] = moist[:, t * LOCAL : (t + 1) * LOCAL]
            wet[width // LOCAL + tile] = upper[:, t * LOCAL : (t + 1) * LOCAL]
        dry_state[0, :, where] = snow
        dry_state[1, :, where] = lower
        last_flow[:, where] = 0.45 * moist * inv_cap

    for k in range(5, 10):
        whole_copy(k).wait()
    slots = lanes_of(position[...])
    pick = (lax.broadcasted_iota(jnp.int32, (NB, LOCAL), 0) == slots).astype(jnp.bfloat16)
    blocks = width // NB
    fields = []
    for b in range(blocks):
        where = pl.ds(b * NB, NB)
        fields += three_parts(flow[hours - 1, :, where]) + three_parts(last_flow[:, where])
    taken = jnp.dot(jnp.concatenate(fields, axis=0), pick, preferred_element_type=jnp.float32)
    lane = lax.broadcasted_iota(jnp.int32, (members, LOCAL), 1)
    predicted = jnp.zeros((members, LOCAL), jnp.float32)
    for b in range(blocks):
        part6 = [taken[(b * 6 + k) * members : (b * 6 + k + 1) * members] for k in range(6)]
        gauge = (part6[2] + part6[1]) + part6[0]
        smap = (part6[5] + part6[4]) + part6[3]
        chosen = jnp.where(lane % OBS < OBS // 2, gauge, smap)
        predicted = jnp.where(lane // OBS == b, chosen, predicted)
    sd = lanes_of(sigma[...])
    spread = jnp.concatenate([draws[b] for b in range(blocks)], axis=1)
    pred[...] = predicted
    wet[wet.shape[0] - 1] = predicted
    fixed[0:members] = lanes_of(measured[...]) + sd * spread
    fixed[members:] = jnp.broadcast_to(
        lanes_of(present[...].astype(jnp.float32)) / sd, (fixed.shape[0] - members, LOCAL)
    )


def forecast(*arrays):
    hours, members, width = arrays[2].shape
    copies = (width // min(STRIP, width)) * (hours // CHUNK)
    f32 = jnp.float32
    vmem = pl.BlockSpec(memory_space=pltpu.VMEM)
    hbm = pl.BlockSpec(memory_space=pltpu.HBM)
    return pl.pallas_call(
        forecast_kernel,
        out_shape=(
            pltpu.VMEM((hours, members, width), f32),
            jax.ShapeDtypeStruct((2 * width // LOCAL + 1, members, LOCAL), f32),
            jax.ShapeDtypeStruct((2, members, width), f32),
            jax.ShapeDtypeStruct((members, LOCAL), f32),
            jax.ShapeDtypeStruct((members + 8, LOCAL), f32),
        ),
        in_specs=[hbm] * len(arrays),
        out_specs=(vmem, vmem, vmem, vmem, vmem),
        scratch_shapes=[pltpu.VMEM(x.shape, x.dtype) for x in arrays]
        + [
            pltpu.VMEM((hours, width), f32),
            pltpu.VMEM((hours, width), f32),
            pltpu.VMEM((members, width), f32),
            pltpu.SemaphoreType.DMA((len(arrays),)),
            pltpu.SemaphoreType.DMA((copies,)),
        ],
        compiler_params=pltpu.CompilerParams(vmem_limit_bytes=VMEM_LIMIT),
        name="forecast",
    )(*(pltpu.with_memory_space_constraint(x, pltpu.HBM) for x in arrays))


def spread_lane(x, k):
    where = jnp.full((8, LOCAL), k, jnp.int32)
    return jnp.take_along_axis(x, where, axis=1, mode="promise_in_bounds")


def spread_row(x, k):
    return jnp.broadcast_to(x[k : k + 1], (8, LOCAL))


def reduce_rows(rows, first):
    sub = lax.broadcasted_iota(jnp.int32, (8, LOCAL), 0)
    columns = [spread_lane(rows, first + j) for j in range(8)]
    for j in range(8):
        inverse = 1.0 / spread_row(columns[j], j)
        for i in range(j + 1, 8):
            scaled = spread_row(columns[i], j) * inverse
            columns[i] = jnp.where(sub == j, scaled, columns[i] - columns[j] * scaled)
        scaled = spread_row(rows, j) * inverse
        rows = jnp.where(sub == j, scaled, rows - columns[j] * scaled)
    return rows


def solve(systems):
    size = systems[0].shape[0]
    half = size // 2
    groups = half // 8

    def reduce_half(mats, first):
        mats = [[m[g * 8 : g * 8 + 8] for g in range(groups)] for m in mats]
        for p in range(groups):
            for mat in mats:
                at = first + p * 8
                mat[p] = reduce_rows(mat[p], at)
                rows = [spread_row(mat[p], j) for j in range(8)]
                for g in range(groups):
                    if g != p:
                        terms = [spread_lane(mat[g], at + j) * rows[j] for j in range(8)]
                        while len(terms) > 1:
                            terms = [terms[i] + terms[i + 1] for i in range(0, len(terms), 2)]
                        mat[g] = mat[g] - terms[0]
        return [jnp.concatenate(mat, axis=0) for mat in mats]

    def minus(x, left, right):
        return x - jnp.dot(left, right, precision=HIGHEST, preferred_element_type=jnp.float32)

    tops = reduce_half([m[:half] for m in systems], 0)
    lows = [minus(m[half:], m[half:, :half], top) for m, top in zip(systems, tops)]
    lows = reduce_half(lows, half)
    tops = [minus(top, top[:, half:size], low) for top, low in zip(tops, lows)]
    return [jnp.concatenate([top, low], axis=0) for top, low in zip(tops, lows)]


def gain_kernel(total, count, relative, index, adjacency, *refs):
    pieces, (gain_out, table) = refs[:count], refs[count:]
    at = 0
    for piece in pieces:
        table[at : at + piece.shape[0]] = piece[...]
        at += piece.shape[0]
    me = index[0]
    blocks, members, _ = gain_out.shape
    rows = table.shape[1]
    lane = lax.broadcasted_iota(jnp.int32, (rows, LOCAL), 1) // OBS
    systems = []
    for b in range(blocks):
        local = jnp.zeros((rows, LOCAL), jnp.float32)
        for i in range(NBR + 1):
            source = me * blocks + b if i == 0 else adjacency[i - 1, me * blocks + b]
            owner = source // blocks
            if relative:
                owner = owner ^ me
                far = (owner // 4 + owner // 2 + owner) % 2
                place = (at // 2 - owner // 2) % (at // 2)
                near = table[far * (at // 2) + place]
                far = table[(1 - far) * (at // 2) + place]
                flips = [0] + [k for k in MEMBERS if k < total // members]
                parts = [
                    (near if k in (0,) + MERGE else far)[p * members : (p + 1) * members]
                    for p, k in enumerate(flips)
                ]
                found = jnp.concatenate(parts + [near[total:]], axis=0)
            else:
                found = table[owner]
            shift = ((i + blocks - source % blocks) % blocks) * OBS
            local = jnp.where(lane == i, pltpu.roll(found, shift, 1), local)
        pred, drawn = local[:total], local[total : total + members]
        own = local[:members] if relative else local[total + members : total + 2 * members]
        weight = local[rows - 8 : rows - 7]
        scaled = (pred - jnp.mean(pred, axis=0, keepdims=True)) * weight
        innov = (drawn - own) * weight
        both = jnp.concatenate(
            [scaled, innov, jnp.zeros((LOCAL - total - members, LOCAL), jnp.float32)], axis=0
        )
        matrix = lax.dot_general(
            scaled,
            both,
            (((1,), (1,)), ((), ())),
            precision=HIGHEST,
            preferred_element_type=jnp.float32,
        )
        row = lax.broadcasted_iota(jnp.int32, (total, LOCAL), 0)
        col = lax.broadcasted_iota(jnp.int32, (total, LOCAL), 1)
        systems.append(matrix + jnp.where(row == col, float(total - 1), 0.0))
    solved = solve(systems)
    for b in range(blocks):
        gain = solved[b] - jnp.mean(solved[b], axis=0, keepdims=True)
        gain_out[b] = jnp.transpose(gain)[total : total + members]


def find_gain(pieces, relative, index, adjacency, blocks, members, total):
    vmem = pl.BlockSpec(memory_space=pltpu.VMEM)
    smem = pl.BlockSpec(memory_space=pltpu.SMEM)
    owners = sum(p.shape[0] for p in pieces)
    return pl.pallas_call(
        functools.partial(gain_kernel, total, len(pieces), relative),
        out_shape=jax.ShapeDtypeStruct((blocks, members, total), jnp.float32),
        in_specs=[smem, smem] + [vmem] * len(pieces),
        out_specs=vmem,
        scratch_shapes=[pltpu.VMEM((owners,) + pieces[0].shape[1:], jnp.float32)],
        compiler_params=pltpu.CompilerParams(vmem_limit_bytes=VMEM_LIMIT),
        cost_estimate=pl.CostEstimate(flops=1, bytes_accessed=1, transcendentals=0),
        name="gain",
    )(index, adjacency, *pieces)


def carry_kernel(x, y):
    y[...] = x[...]


def carry(x, cost):
    vmem = pl.BlockSpec(memory_space=pltpu.VMEM)
    return pl.pallas_call(
        carry_kernel,
        out_shape=jax.ShapeDtypeStruct(x.shape, x.dtype),
        in_specs=[vmem],
        out_specs=vmem,
        compiler_params=pltpu.CompilerParams(vmem_limit_bytes=VMEM_LIMIT),
        cost_estimate=pl.CostEstimate(flops=cost, bytes_accessed=0, transcendentals=0),
        name="carry",
    )(x)


def store_kernel(flow, x, flow_hbm, y, sem):
    copy = pltpu.make_async_copy(flow, flow_hbm, sem)
    copy.start()
    y[...] = x[...]
    copy.wait()


def store(flow, x, cost):
    vmem = pl.BlockSpec(memory_space=pltpu.VMEM)
    return pl.pallas_call(
        store_kernel,
        out_shape=(
            jax.ShapeDtypeStruct(flow.shape, flow.dtype),
            jax.ShapeDtypeStruct(x.shape, x.dtype),
        ),
        in_specs=[vmem, vmem],
        out_specs=(pl.BlockSpec(memory_space=pltpu.HBM), vmem),
        scratch_shapes=[pltpu.SemaphoreType.DMA],
        compiler_params=pltpu.CompilerParams(vmem_limit_bytes=VMEM_LIMIT),
        cost_estimate=pl.CostEstimate(flops=cost, bytes_accessed=0, transcendentals=0),
        name="store",
    )(flow, x)


def update_kernel(gain, wet_own, dry, *refs):
    wets, (analysis_hbm, analysis, out_sems) = refs[:-3], refs[-3:]
    blocks = gain.shape[0]

    def out_copy(b):
        where = (slice(None), slice(None), pl.ds(b * NB, NB))
        return pltpu.make_async_copy(analysis.at[where], analysis_hbm.at[where], out_sems.at[b])

    tiles = dry.shape[2] // LOCAL
    for b in range(blocks):
        where = pl.ds(b * NB, NB)
        analysis[:, 0, where] = dry[0, :, where]
        analysis[:, 3, where] = dry[1, :, where]
        for k in range(2):
            at = k * tiles + b * NB // LOCAL
            spots = range(at, at + NB // LOCAL)

            def side(x):
                return jnp.concatenate([x[t] for t in spots], axis=1)

            if len(wets[0].shape) == 3:
                states = [side(wet_own)] + [side(w) for w in wets]
            else:
                states = [jnp.concatenate([w[:, t] for t in spots], axis=2).reshape(-1, NB) for w in wets]
            analysis[:, 1 + k, where] = side(wet_own) + jnp.dot(
                gain[b],
                jnp.concatenate(states, axis=0),
                precision=HIGHEST,
                preferred_element_type=jnp.float32,
            )
        out_copy(b).start()
    for b in range(blocks):
        out_copy(b).wait()


def update(gain, wet, dry, wets):
    _, members, width = dry.shape
    vmem = pl.BlockSpec(memory_space=pltpu.VMEM)
    return pl.pallas_call(
        update_kernel,
        out_shape=jax.ShapeDtypeStruct((members, 4, width), jnp.float32),
        in_specs=[vmem] * (3 + len(wets)),
        out_specs=pl.BlockSpec(memory_space=pltpu.HBM),
        scratch_shapes=[
            pltpu.VMEM((members, 4, width), jnp.float32),
            pltpu.SemaphoreType.DMA((width // NB,)),
        ],
        compiler_params=pltpu.CompilerParams(vmem_limit_bytes=VMEM_LIMIT),
        name="update",
    )(gain, wet, dry, *wets)


def permute(x, axis, mask):
    return lax.ppermute(x, axis, [(i, i ^ mask) for i in range(lax.axis_size(axis))])


def across(x, flip_member):
    basins, members = lax.axis_size("basin"), lax.axis_size("member")
    pairs = [
        (b * members + m, (b ^ 1) * members + (m ^ flip_member))
        for b in range(basins)
        for m in range(members)
    ]
    return lax.ppermute(x, ("basin", "member"), pairs)


def on_device(
    initial_reservoir_levels,
    normalized_catchment_settings,
    rainfall_member_series,
    surface_heat_celsius,
    potential_evapotranspiration,
    gauge_measured_values,
    gauge_deviation_sigma,
    gauge_perturbation_draws,
    gauge_catchment_position,
    gauge_present_flag,
    adjacent_block_list,
):
    members = rainfall_member_series.shape[1]
    blocks = gauge_measured_values.shape[0]
    basin_size, member_size = lax.axis_size("basin"), lax.axis_size("member")
    discharge, wet, dry, pred, fixed = forecast(
        initial_reservoir_levels,
        normalized_catchment_settings,
        rainfall_member_series,
        surface_heat_celsius,
        potential_evapotranspiration,
        gauge_measured_values,
        gauge_deviation_sigma,
        jnp.transpose(gauge_perturbation_draws, (0, 2, 1)),
        gauge_catchment_position,
        gauge_present_flag,
    )
    index = jnp.full((1,), lax.axis_index("basin"), jnp.int32)
    adjacency = jnp.transpose(adjacent_block_list)
    relative = basin_size <= 8 and member_size <= 4
    if relative:
        others = [k for k in MEMBERS if k < member_size]
        first = {k: permute(wet, "member", k) if k in MERGE else across(pred, k) for k in others}
        wets = [first[k] if k in MERGE else permute(wet, "member", k) for k in others]
        preds = [pred] + [first[k][-1] if k in MERGE else first[k] for k in others]
        near = jnp.concatenate(preds + [fixed], axis=0)[None]
        flips = [k for k in range(basin_size - 1, 1, -1) if k in (3, 5, 6)]
        near = jnp.concatenate([near] + [permute(near, "basin", k) for k in flips], axis=0)
        packs = [near, permute(near, "basin", 1)]
        discharge, dry = store(discharge, dry, COSTS[0])
        dry = carry(dry, COSTS[1])
    else:
        preds = lax.all_gather(pred, "member", axis=0).reshape(-1, LOCAL)
        wets = [lax.all_gather(wet, "member", axis=0)]
        mine = jnp.concatenate([preds, fixed[:members], pred, fixed[members:]], axis=0)
        packs = [lax.all_gather(mine, "basin", axis=0)]
    gain = find_gain(
        packs, relative, index, adjacency, blocks, members, members * member_size
    )
    analysis = update(gain, wet, dry, wets)
    return (analysis, discharge)


def solution(mesh):
    placed = (
        P("member", None, "basin"),
        P(None, "basin"),
        P(None, "member", "basin"),
        P(None, "basin"),
        P(None, "basin"),
        P("basin", None),
        P("basin", None),
        P("basin", None, "member"),
        P("basin", None),
        P("basin", None),
        P(),
    )
    return jax.shard_map(
        on_device,
        mesh=mesh,
        in_specs=placed,
        out_specs=(P("member", None, "basin"), P(None, "member", "basin")),
        check_vma=False,
    )
```

```python
import functools

import jax
import jax.numpy as jnp
from jax import lax
from jax.experimental import pallas as pl
from jax.experimental.pallas import tpu as pltpu
from jax.sharding import PartitionSpec as P

NB = 256
OBS = 32
NBR = 3
LOCAL = 128

PARAM_LOW = (-1.5, 0.0002, 0.8, 1.0, 0.4, 0.01, 0.002, 0.0001, 0.1, 0.0001)
PARAM_HIGH = (1.5, 0.002, 4.0, 5.0, 1.0, 0.05, 0.02, 0.002, 0.5, 0.001)

HIGHEST = lax.Precision.HIGHEST
STRIP = 512
COSTS = (10**10, 10**10)
MERGE = (1,)
MEMBERS = (1, 3, 2)
CHUNK = 8
PACK = 40
VMEM_LIMIT = 16 * 1024 * 1024


def lanes_of(table):
    return jnp.concatenate([table[b : b + 1] for b in range(table.shape[0])], axis=1)


def three_parts(x):
    high = x.astype(jnp.bfloat16)
    rest = x - high.astype(jnp.float32)
    middle = rest.astype(jnp.bfloat16)
    low = (rest - middle.astype(jnp.float32)).astype(jnp.bfloat16)
    return [high, middle, low]


def forecast_kernel(*refs):
    inputs, (flow, wet, dry_state, pred, fixed) = refs[:10], refs[10:15]
    held, (share, melt_cap, last_flow, held_sems, in_sems) = refs[15:25], refs[25:]
    levels, settings, rain, heat, evap, measured, sigma, draws, position, present = held
    rain_hbm = inputs[2]
    hours, members, width = rain.shape
    strip = min(STRIP, width)
    pieces = [(s, c) for s in range(width // strip) for c in range(hours // CHUNK)]

    def part(s, c):
        return (pl.ds(c * CHUNK, CHUNK), slice(None), pl.ds(s * strip, strip))

    def whole_copy(k):
        return pltpu.make_async_copy(inputs[k], held[k], held_sems.at[k])

    def rain_copy(n):
        where = part(*pieces[n])
        return pltpu.make_async_copy(rain_hbm.at[where], rain.at[where], in_sems.at[n])

    for k in (1, 3, 4, 0):
        whole_copy(k).start()
    for n in range(len(pieces)):
        rain_copy(n).start()
    for k in range(5, 10):
        whole_copy(k).start()

    def parameter(k, where=slice(None)):
        return PARAM_LOW[k] + (PARAM_HIGH[k] - PARAM_LOW[k]) * settings[k : k + 1, where]

    whole_copy(1).wait()
    whole_copy(3).wait()
    share[...] = jnp.clip((parameter(0) + 1.0 - heat[...]) * 0.5, 0.0, 1.0)
    melt_cap[...] = parameter(1) * jnp.maximum(heat[...] - parameter(0), 0.0)
    whole_copy(4).wait()
    whole_copy(0).wait()

    for s in range(width // strip):
        where = pl.ds(s * strip, strip)
        field_cap = parameter(2, where)
        inv_cap = 1.0 / field_cap
        shape_exp = parameter(3, where)
        inv_limit = 1.0 / (parameter(4, where) * field_cap)
        quick_rate, upper_rate, lower_rate, upper_limit, percolation = (
            parameter(k, where) for k in range(5, 10)
        )
        state = tuple(levels[:, k, where] for k in range(4))

        def hour(h, state):
            snow, moist, upper, lower = state
            fall = rain[h, :, where]
            snow_fall = share[pl.ds(h, 1), where] * fall
            snow = snow + snow_fall
            melt = jnp.minimum(melt_cap[pl.ds(h, 1), where], snow)
            snow = snow - melt
            inflow = (fall - snow_fall) + melt
            recharge = inflow * jnp.exp2(shape_exp * jnp.log2(moist * inv_cap))
            moist = moist + inflow - recharge
            excess = jnp.maximum(moist - field_cap, 0.0)
            moist = moist - excess
            actual = jnp.minimum(
                evap[pl.ds(h, 1), where] * jnp.minimum(moist * inv_limit, 1.0), moist
            )
            moist = moist - actual
            upper = upper + recharge + excess
            perc_flow = jnp.minimum(percolation, upper)
            upper = upper - perc_flow
            lower = lower + perc_flow
            fast = quick_rate * jnp.maximum(upper - upper_limit, 0.0) + upper_rate * upper
            base = lower_rate * lower
            upper = upper - fast
            lower = lower - base
            flow[h, :, where] = 100.0 * (fast + base)
            return (snow, moist, upper, lower)

        for c in range(hours // CHUNK):
            n = s * (hours // CHUNK) + c
            rain_copy(n).wait()
            state = lax.fori_loop(c * CHUNK, (c + 1) * CHUNK, hour, state, unroll=CHUNK)
        snow, moist, upper, lower = state
        for t in range(strip // LOCAL):
            tile = s * (strip // LOCAL) + t
            wet[tile] = moist[:, t * LOCAL : (t + 1) * LOCAL]
            wet[width // LOCAL + tile] = upper[:, t * LOCAL : (t + 1) * LOCAL]
        dry_state[0, :, where] = snow
        dry_state[1, :, where] = lower
        last_flow[:, where] = 0.45 * moist * inv_cap

    for k in range(5, 10):
        whole_copy(k).wait()
    slots = lanes_of(position[...])
    pick = (lax.broadcasted_iota(jnp.int32, (NB, LOCAL), 0) == slots).astype(jnp.bfloat16)
    blocks = width // NB
    fields = []
    for b in range(blocks):
        where = pl.ds(b * NB, NB)
        fields += three_parts(flow[hours - 1, :, where]) + three_parts(last_flow[:, where])
    taken = jnp.dot(jnp.concatenate(fields, axis=0), pick, preferred_element_type=jnp.float32)
    lane = lax.broadcasted_iota(jnp.int32, (members, LOCAL), 1)
    predicted = jnp.zeros((members, LOCAL), jnp.float32)
    for b in range(blocks):
        part6 = [taken[(b * 6 + k) * members : (b * 6 + k + 1) * members] for k in range(6)]
        gauge = (part6[2] + part6[1]) + part6[0]
        smap = (part6[5] + part6[4]) + part6[3]
        chosen = jnp.where(lane % OBS < OBS // 2, gauge, smap)
        predicted = jnp.where(lane // OBS == b, chosen, predicted)
    sd = lanes_of(sigma[...])
    spread = jnp.concatenate([draws[b] for b in range(blocks)], axis=1)
    pred[...] = predicted
    wet[wet.shape[0] - 1] = predicted
    fixed[0:members] = lanes_of(measured[...]) + sd * spread
    fixed[members:] = jnp.broadcast_to(
        lanes_of(present[...].astype(jnp.float32)) / sd, (fixed.shape[0] - members, LOCAL)
    )


def forecast(*arrays):
    hours, members, width = arrays[2].shape
    copies = (width // min(STRIP, width)) * (hours // CHUNK)
    f32 = jnp.float32
    vmem = pl.BlockSpec(memory_space=pltpu.VMEM)
    hbm = pl.BlockSpec(memory_space=pltpu.HBM)
    return pl.pallas_call(
        forecast_kernel,
        out_shape=(
            pltpu.VMEM((hours, members, width), f32),
            jax.ShapeDtypeStruct((2 * width // LOCAL + 1, members, LOCAL), f32),
            jax.ShapeDtypeStruct((2, members, width), f32),
            jax.ShapeDtypeStruct((members, LOCAL), f32),
            jax.ShapeDtypeStruct((members + 8, LOCAL), f32),
        ),
        in_specs=[hbm] * len(arrays),
        out_specs=(vmem, vmem, vmem, vmem, vmem),
        scratch_shapes=[pltpu.VMEM(x.shape, x.dtype) for x in arrays]
        + [
            pltpu.VMEM((hours, width), f32),
            pltpu.VMEM((hours, width), f32),
            pltpu.VMEM((members, width), f32),
            pltpu.SemaphoreType.DMA((len(arrays),)),
            pltpu.SemaphoreType.DMA((copies,)),
        ],
        compiler_params=pltpu.CompilerParams(vmem_limit_bytes=VMEM_LIMIT),
        name="forecast",
    )(*(pltpu.with_memory_space_constraint(x, pltpu.HBM) for x in arrays))


def spread_lane(x, k):
    where = jnp.full((8, LOCAL), k, jnp.int32)
    return jnp.take_along_axis(x, where, axis=1, mode="promise_in_bounds")


def spread_row(x, k):
    return jnp.broadcast_to(x[k : k + 1], (8, LOCAL))


def reduce_rows(rows, first):
    sub = lax.broadcasted_iota(jnp.int32, (8, LOCAL), 0)
    columns = [spread_lane(rows, first + j) for j in range(8)]
    for j in range(8):
        inverse = 1.0 / spread_row(columns[j], j)
        for i in range(j + 1, 8):
            scaled = spread_row(columns[i], j) * inverse
            columns[i] = jnp.where(sub == j, scaled, columns[i] - columns[j] * scaled)
        scaled = spread_row(rows, j) * inverse
        rows = jnp.where(sub == j, scaled, rows - columns[j] * scaled)
    return rows


def solve(systems):
    size = systems[0].shape[0]
    half = size // 2
    groups = half // 8

    def reduce_half(mats, first):
        mats = [[m[g * 8 : g * 8 + 8] for g in range(groups)] for m in mats]
        for p in range(groups):
            for mat in mats:
                at = first + p * 8
                mat[p] = reduce_rows(mat[p], at)
                rows = [spread_row(mat[p], j) for j in range(8)]
                for g in range(groups):
                    if g != p:
                        terms = [spread_lane(mat[g], at + j) * rows[j] for j in range(8)]
                        while len(terms) > 1:
                            terms = [terms[i] + terms[i + 1] for i in range(0, len(terms), 2)]
                        mat[g] = mat[g] - terms[0]
        return [jnp.concatenate(mat, axis=0) for mat in mats]

    def minus(x, left, right):
        return x - jnp.dot(left, right, precision=HIGHEST, preferred_element_type=jnp.float32)

    tops = reduce_half([m[:half] for m in systems], 0)
    lows = [minus(m[half:], m[half:, :half], top) for m, top in zip(systems, tops)]
    lows = reduce_half(lows, half)
    tops = [minus(top, top[:, half:size], low) for top, low in zip(tops, lows)]
    return [jnp.concatenate([top, low], axis=0) for top, low in zip(tops, lows)]


def gain_kernel(total, count, relative, index, adjacency, *refs):
    pieces, gain_out = refs[:count], refs[count]
    chips = pieces[0].shape[0]
    me = index[0]
    blocks, members, _ = gain_out.shape
    rows = pieces[0].shape[1]
    lane = lax.broadcasted_iota(jnp.int32, (rows, LOCAL), 1) // OBS
    systems = []
    for b in range(blocks):
        local = jnp.zeros((rows, LOCAL), jnp.float32)
        for i in range(NBR + 1):
            source = me * blocks + b if i == 0 else adjacency[i - 1, me * blocks + b]
            owner = source // blocks
            if relative:
                owner = owner ^ me
                far = (owner // 4 + owner // 2 + owner) % 2
                place = (chips - owner // 2) % chips
                here, there = pieces[0][place], pieces[1][place]
                near, far = jnp.where(far == 0, here, there), jnp.where(far == 0, there, here)
                flips = [0] + [k for k in MEMBERS if k < total // members]
                parts = [
                    (near if k in (0,) + MERGE else far)[p * members : (p + 1) * members]
                    for p, k in enumerate(flips)
                ]
                found = jnp.concatenate(parts + [near[total:]], axis=0)
            else:
                found = pieces[0][owner]
            shift = ((i + blocks - source % blocks) % blocks) * OBS
            local = jnp.where(lane == i, pltpu.roll(found, shift, 1), local)
        pred, drawn = local[:total], local[total : total + members]
        own = local[:members] if relative else local[total + members : total + 2 * members]
        weight = local[rows - 8 : rows - 7]
        scaled = (pred - jnp.mean(pred, axis=0, keepdims=True)) * weight
        innov = (drawn - own) * weight
        both = jnp.concatenate(
            [scaled, innov, jnp.zeros((LOCAL - total - members, LOCAL), jnp.float32)], axis=0
        )
        matrix = lax.dot_general(
            scaled,
            both,
            (((1,), (1,)), ((), ())),
            precision=HIGHEST,
            preferred_element_type=jnp.float32,
        )
        row = lax.broadcasted_iota(jnp.int32, (total, LOCAL), 0)
        col = lax.broadcasted_iota(jnp.int32, (total, LOCAL), 1)
        systems.append(matrix + jnp.where(row == col, float(total - 1), 0.0))
    solved = solve(systems)
    for b in range(blocks):
        gain = solved[b] - jnp.mean(solved[b], axis=0, keepdims=True)
        gain_out[b] = jnp.transpose(gain)[total : total + members]


def find_gain(pieces, relative, index, adjacency, blocks, members, total):
    vmem = pl.BlockSpec(memory_space=pltpu.VMEM)
    smem = pl.BlockSpec(memory_space=pltpu.SMEM)
    return pl.pallas_call(
        functools.partial(gain_kernel, total, len(pieces), relative),
        out_shape=jax.ShapeDtypeStruct((blocks, members, total), jnp.float32),
        in_specs=[smem, smem] + [vmem] * len(pieces),
        out_specs=vmem,
        compiler_params=pltpu.CompilerParams(vmem_limit_bytes=VMEM_LIMIT),
        cost_estimate=pl.CostEstimate(flops=1, bytes_accessed=1, transcendentals=0),
        name="gain",
    )(index, adjacency, *pieces)


def carry_kernel(x, y):
    y[...] = x[...]


def carry(x, cost):
    vmem = pl.BlockSpec(memory_space=pltpu.VMEM)
    return pl.pallas_call(
        carry_kernel,
        out_shape=jax.ShapeDtypeStruct(x.shape, x.dtype),
        in_specs=[vmem],
        out_specs=vmem,
        compiler_params=pltpu.CompilerParams(vmem_limit_bytes=VMEM_LIMIT),
        cost_estimate=pl.CostEstimate(flops=cost, bytes_accessed=0, transcendentals=0),
        name="carry",
    )(x)


def store_kernel(flow, x, flow_hbm, y, sem):
    copy = pltpu.make_async_copy(flow, flow_hbm, sem)
    copy.start()
    y[...] = x[...]
    copy.wait()


def store(flow, x, cost):
    vmem = pl.BlockSpec(memory_space=pltpu.VMEM)
    return pl.pallas_call(
        store_kernel,
        out_shape=(
            jax.ShapeDtypeStruct(flow.shape, flow.dtype),
            jax.ShapeDtypeStruct(x.shape, x.dtype),
        ),
        in_specs=[vmem, vmem],
        out_specs=(pl.BlockSpec(memory_space=pltpu.HBM), vmem),
        scratch_shapes=[pltpu.SemaphoreType.DMA],
        compiler_params=pltpu.CompilerParams(vmem_limit_bytes=VMEM_LIMIT),
        cost_estimate=pl.CostEstimate(flops=cost, bytes_accessed=0, transcendentals=0),
        name="store",
    )(flow, x)


def update_kernel(gain, wet_own, dry, *refs):
    wets, (analysis_hbm, analysis, out_sems) = refs[:-3], refs[-3:]
    blocks = gain.shape[0]

    def out_copy(b):
        where = (slice(None), slice(None), pl.ds(b * NB, NB))
        return pltpu.make_async_copy(analysis.at[where], analysis_hbm.at[where], out_sems.at[b])

    tiles = dry.shape[2] // LOCAL
    for b in range(blocks):
        where = pl.ds(b * NB, NB)
        analysis[:, 0, where] = dry[0, :, where]
        analysis[:, 3, where] = dry[1, :, where]
        for k in range(2):
            at = k * tiles + b * NB // LOCAL
            spots = range(at, at + NB // LOCAL)

            def side(x):
                return jnp.concatenate([x[t] for t in spots], axis=1)

            if len(wets[0].shape) == 3:
                states = [side(wet_own)] + [side(w) for w in wets]
            else:
                states = [jnp.concatenate([w[:, t] for t in spots], axis=2).reshape(-1, NB) for w in wets]
            analysis[:, 1 + k, where] = side(wet_own) + jnp.dot(
                gain[b],
                jnp.concatenate(states, axis=0),
                precision=HIGHEST,
                preferred_element_type=jnp.float32,
            )
        out_copy(b).start()
    for b in range(blocks):
        out_copy(b).wait()


def update(gain, wet, dry, wets):
    _, members, width = dry.shape
    vmem = pl.BlockSpec(memory_space=pltpu.VMEM)
    return pl.pallas_call(
        update_kernel,
        out_shape=jax.ShapeDtypeStruct((members, 4, width), jnp.float32),
        in_specs=[vmem] * (3 + len(wets)),
        out_specs=pl.BlockSpec(memory_space=pltpu.HBM),
        scratch_shapes=[
            pltpu.VMEM((members, 4, width), jnp.float32),
            pltpu.SemaphoreType.DMA((width // NB,)),
        ],
        compiler_params=pltpu.CompilerParams(vmem_limit_bytes=VMEM_LIMIT),
        name="update",
    )(gain, wet, dry, *wets)


def permute(x, axis, mask):
    return lax.ppermute(x, axis, [(i, i ^ mask) for i in range(lax.axis_size(axis))])


def across(x, flip_member):
    basins, members = lax.axis_size("basin"), lax.axis_size("member")
    pairs = [
        (b * members + m, (b ^ 1) * members + (m ^ flip_member))
        for b in range(basins)
        for m in range(members)
    ]
    return lax.ppermute(x, ("basin", "member"), pairs)


def on_device(
    initial_reservoir_levels,
    normalized_catchment_settings,
    rainfall_member_series,
    surface_heat_celsius,
    potential_evapotranspiration,
    gauge_measured_values,
    gauge_deviation_sigma,
    gauge_perturbation_draws,
    gauge_catchment_position,
    gauge_present_flag,
    adjacent_block_list,
):
    members = rainfall_member_series.shape[1]
    blocks = gauge_measured_values.shape[0]
    basin_size, member_size = lax.axis_size("basin"), lax.axis_size("member")
    discharge, wet, dry, pred, fixed = forecast(
        initial_reservoir_levels,
        normalized_catchment_settings,
        rainfall_member_series,
        surface_heat_celsius,
        potential_evapotranspiration,
        gauge_measured_values,
        gauge_deviation_sigma,
        jnp.transpose(gauge_perturbation_draws, (0, 2, 1)),
        gauge_catchment_position,
        gauge_present_flag,
    )
    index = jnp.full((1,), lax.axis_index("basin"), jnp.int32)
    adjacency = jnp.transpose(adjacent_block_list)
    relative = basin_size <= 8 and member_size <= 4
    if relative:
        others = [k for k in MEMBERS if k < member_size]
        first = {k: permute(wet, "member", k) if k in MERGE else across(pred, k) for k in others}
        wets = [first[k] if k in MERGE else permute(wet, "member", k) for k in others]
        preds = [pred] + [first[k][-1] if k in MERGE else first[k] for k in others]
        near = jnp.concatenate(preds + [fixed], axis=0)[None]
        flips = [k for k in range(basin_size - 1, 1, -1) if k in (3, 5, 6)]
        near = jnp.concatenate([near] + [permute(near, "basin", k) for k in flips], axis=0)
        packs = [near, permute(near, "basin", 1)]
        discharge, dry = store(discharge, dry, COSTS[0])
        dry = carry(dry, COSTS[1])
    else:
        preds = lax.all_gather(pred, "member", axis=0).reshape(-1, LOCAL)
        wets = [lax.all_gather(wet, "member", axis=0)]
        mine = jnp.concatenate([preds, fixed[:members], pred, fixed[members:]], axis=0)
        packs = [lax.all_gather(mine, "basin", axis=0)]
    gain = find_gain(
        packs, relative, index, adjacency, blocks, members, members * member_size
    )
    analysis = update(gain, wet, dry, wets)
    return (analysis, discharge)


def solution(mesh):
    placed = (
        P("member", None, "basin"),
        P(None, "basin"),
        P(None, "member", "basin"),
        P(None, "basin"),
        P(None, "basin"),
        P("basin", None),
        P("basin", None),
        P("basin", None, "member"),
        P("basin", None),
        P("basin", None),
        P(),
    )
    return jax.shard_map(
        on_device,
        mesh=mesh,
        in_specs=placed,
        out_specs=(P("member", None, "basin"), P(None, "member", "basin")),
        check_vma=False,
    )
```

```python
import functools

import jax
import jax.numpy as jnp
from jax import lax
from jax.experimental import pallas as pl
from jax.experimental.pallas import tpu as pltpu
from jax.sharding import PartitionSpec as P

NB = 256
OBS = 32
NBR = 3
LOCAL = 128

PARAM_LOW = (-1.5, 0.0002, 0.8, 1.0, 0.4, 0.01, 0.002, 0.0001, 0.1, 0.0001)
PARAM_HIGH = (1.5, 0.002, 4.0, 5.0, 1.0, 0.05, 0.02, 0.002, 0.5, 0.001)

HIGHEST = lax.Precision.HIGHEST
STRIP = 512
COSTS = (10**10, 10**10)
MERGE = (1,)
MEMBERS = (1, 3, 2)
CHUNK = 8
PACK = 40
VMEM_LIMIT = 16 * 1024 * 1024


def lanes_of(table):
    return jnp.concatenate([table[b : b + 1] for b in range(table.shape[0])], axis=1)


def three_parts(x):
    high = x.astype(jnp.bfloat16)
    rest = x - high.astype(jnp.float32)
    middle = rest.astype(jnp.bfloat16)
    low = (rest - middle.astype(jnp.float32)).astype(jnp.bfloat16)
    return [high, middle, low]


def forecast_kernel(*refs):
    inputs, (flow, wet, dry_state, pred, fixed) = refs[:10], refs[10:15]
    held, (share, melt_cap, last_flow, held_sems, in_sems) = refs[15:25], refs[25:]
    levels, settings, rain, heat, evap, measured, sigma, draws, position, present = held
    rain_hbm = inputs[2]
    hours, members, width = rain.shape
    strip = min(STRIP, width)
    pieces = [(s, c) for s in range(width // strip) for c in range(hours // CHUNK)]

    def part(s, c):
        return (pl.ds(c * CHUNK, CHUNK), slice(None), pl.ds(s * strip, strip))

    def whole_copy(k):
        return pltpu.make_async_copy(inputs[k], held[k], held_sems.at[k])

    def rain_copy(n):
        where = part(*pieces[n])
        return pltpu.make_async_copy(rain_hbm.at[where], rain.at[where], in_sems.at[n])

    for k in (1, 3, 4, 0):
        whole_copy(k).start()
    for n in range(len(pieces)):
        rain_copy(n).start()
    for k in range(5, 10):
        whole_copy(k).start()

    def parameter(k, where=slice(None)):
        return PARAM_LOW[k] + (PARAM_HIGH[k] - PARAM_LOW[k]) * settings[k : k + 1, where]

    whole_copy(1).wait()
    whole_copy(3).wait()
    share[...] = jnp.clip((parameter(0) + 1.0 - heat[...]) * 0.5, 0.0, 1.0)
    melt_cap[...] = parameter(1) * jnp.maximum(heat[...] - parameter(0), 0.0)
    whole_copy(4).wait()
    whole_copy(0).wait()

    for s in range(width // strip):
        where = pl.ds(s * strip, strip)
        field_cap = parameter(2, where)
        inv_cap = 1.0 / field_cap
        shape_exp = parameter(3, where)
        inv_limit = 1.0 / (parameter(4, where) * field_cap)
        quick_rate, upper_rate, lower_rate, upper_limit, percolation = (
            parameter(k, where) for k in range(5, 10)
        )
        state = tuple(levels[:, k, where] for k in range(4))

        def hour(h, state):
            snow, moist, upper, lower = state
            fall = rain[h, :, where]
            snow_fall = share[pl.ds(h, 1), where] * fall
            snow = snow + snow_fall
            cap = melt_cap[pl.ds(h, 1), where]
            melt = jnp.minimum(cap, snow)
            snow = jnp.maximum(snow - cap, 0.0)
            inflow = (fall - snow_fall) + melt
            recharge = inflow * jnp.exp2(shape_exp * jnp.log2(moist * inv_cap))
            moist = moist + inflow - recharge
            excess = jnp.maximum(moist - field_cap, 0.0)
            moist = jnp.minimum(moist, field_cap)
            demand = evap[pl.ds(h, 1), where] * jnp.minimum(moist * inv_limit, 1.0)
            moist = jnp.maximum(moist - demand, 0.0)
            upper = upper + recharge + excess
            perc_flow = jnp.minimum(percolation, upper)
            upper = jnp.maximum(upper - percolation, 0.0)
            lower = lower + perc_flow
            fast = quick_rate * jnp.maximum(upper - upper_limit, 0.0) + upper_rate * upper
            base = lower_rate * lower
            upper = upper - fast
            lower = lower - base
            flow[h, :, where] = 100.0 * (fast + base)
            return (snow, moist, upper, lower)

        for c in range(hours // CHUNK):
            n = s * (hours // CHUNK) + c
            rain_copy(n).wait()
            state = lax.fori_loop(c * CHUNK, (c + 1) * CHUNK, hour, state, unroll=CHUNK)
        snow, moist, upper, lower = state
        for t in range(strip // LOCAL):
            tile = s * (strip // LOCAL) + t
            wet[tile] = moist[:, t * LOCAL : (t + 1) * LOCAL]
            wet[width // LOCAL + tile] = upper[:, t * LOCAL : (t + 1) * LOCAL]
        dry_state[0, :, where] = snow
        dry_state[1, :, where] = lower
        last_flow[:, where] = 0.45 * moist * inv_cap

    for k in range(5, 10):
        whole_copy(k).wait()
    slots = lanes_of(position[...])
    pick = (lax.broadcasted_iota(jnp.int32, (NB, LOCAL), 0) == slots).astype(jnp.bfloat16)
    blocks = width // NB
    fields = []
    for b in range(blocks):
        where = pl.ds(b * NB, NB)
        fields += three_parts(flow[hours - 1, :, where]) + three_parts(last_flow[:, where])
    taken = jnp.dot(jnp.concatenate(fields, axis=0), pick, preferred_element_type=jnp.float32)
    lane = lax.broadcasted_iota(jnp.int32, (members, LOCAL), 1)
    predicted = jnp.zeros((members, LOCAL), jnp.float32)
    for b in range(blocks):
        part6 = [taken[(b * 6 + k) * members : (b * 6 + k + 1) * members] for k in range(6)]
        gauge = (part6[2] + part6[1]) + part6[0]
        smap = (part6[5] + part6[4]) + part6[3]
        chosen = jnp.where(lane % OBS < OBS // 2, gauge, smap)
        predicted = jnp.where(lane // OBS == b, chosen, predicted)
    sd = lanes_of(sigma[...])
    spread = jnp.concatenate([draws[b] for b in range(blocks)], axis=1)
    pred[...] = predicted
    wet[wet.shape[0] - 1] = predicted
    fixed[0:members] = lanes_of(measured[...]) + sd * spread
    fixed[members:] = jnp.broadcast_to(
        lanes_of(present[...].astype(jnp.float32)) / sd, (fixed.shape[0] - members, LOCAL)
    )


def forecast(*arrays):
    hours, members, width = arrays[2].shape
    copies = (width // min(STRIP, width)) * (hours // CHUNK)
    f32 = jnp.float32
    vmem = pl.BlockSpec(memory_space=pltpu.VMEM)
    hbm = pl.BlockSpec(memory_space=pltpu.HBM)
    return pl.pallas_call(
        forecast_kernel,
        out_shape=(
            pltpu.VMEM((hours, members, width), f32),
            jax.ShapeDtypeStruct((2 * width // LOCAL + 1, members, LOCAL), f32),
            jax.ShapeDtypeStruct((2, members, width), f32),
            jax.ShapeDtypeStruct((members, LOCAL), f32),
            jax.ShapeDtypeStruct((members + 8, LOCAL), f32),
        ),
        in_specs=[hbm] * len(arrays),
        out_specs=(vmem, vmem, vmem, vmem, vmem),
        scratch_shapes=[pltpu.VMEM(x.shape, x.dtype) for x in arrays]
        + [
            pltpu.VMEM((hours, width), f32),
            pltpu.VMEM((hours, width), f32),
            pltpu.VMEM((members, width), f32),
            pltpu.SemaphoreType.DMA((len(arrays),)),
            pltpu.SemaphoreType.DMA((copies,)),
        ],
        compiler_params=pltpu.CompilerParams(vmem_limit_bytes=VMEM_LIMIT),
        name="forecast",
    )(*(pltpu.with_memory_space_constraint(x, pltpu.HBM) for x in arrays))


def spread_lane(x, k):
    where = jnp.full((8, LOCAL), k, jnp.int32)
    return jnp.take_along_axis(x, where, axis=1, mode="promise_in_bounds")


def spread_row(x, k):
    return jnp.broadcast_to(x[k : k + 1], (8, LOCAL))


def reduce_rows(rows, first):
    sub = lax.broadcasted_iota(jnp.int32, (8, LOCAL), 0)
    columns = [spread_lane(rows, first + j) for j in range(8)]
    for j in range(8):
        inverse = 1.0 / spread_row(columns[j], j)
        for i in range(j + 1, 8):
            scaled = spread_row(columns[i], j) * inverse
            columns[i] = jnp.where(sub == j, scaled, columns[i] - columns[j] * scaled)
        scaled = spread_row(rows, j) * inverse
        rows = jnp.where(sub == j, scaled, rows - columns[j] * scaled)
    return rows


def solve(systems):
    size = systems[0].shape[0]
    half = size // 2
    groups = half // 8

    def reduce_half(mats, first):
        mats = [[m[g * 8 : g * 8 + 8] for g in range(groups)] for m in mats]
        for p in range(groups):
            for mat in mats:
                at = first + p * 8
                mat[p] = reduce_rows(mat[p], at)
                rows = [spread_row(mat[p], j) for j in range(8)]
                for g in range(groups):
                    if g != p:
                        terms = [spread_lane(mat[g], at + j) * rows[j] for j in range(8)]
                        while len(terms) > 1:
                            terms = [terms[i] + terms[i + 1] for i in range(0, len(terms), 2)]
                        mat[g] = mat[g] - terms[0]
        return [jnp.concatenate(mat, axis=0) for mat in mats]

    def minus(x, left, right):
        return x - jnp.dot(left, right, precision=HIGHEST, preferred_element_type=jnp.float32)

    tops = reduce_half([m[:half] for m in systems], 0)
    lows = [minus(m[half:], m[half:, :half], top) for m, top in zip(systems, tops)]
    lows = reduce_half(lows, half)
    tops = [minus(top, top[:, half:size], low) for top, low in zip(tops, lows)]
    return [jnp.concatenate([top, low], axis=0) for top, low in zip(tops, lows)]


def gain_kernel(total, count, relative, index, adjacency, *refs):
    pieces, gain_out = refs[:count], refs[count]
    chips = pieces[0].shape[0]
    me = index[0]
    blocks, members, _ = gain_out.shape
    rows = pieces[0].shape[1]
    lane = lax.broadcasted_iota(jnp.int32, (rows, LOCAL), 1) // OBS
    systems = []
    for b in range(blocks):
        local = jnp.zeros((rows, LOCAL), jnp.float32)
        for i in range(NBR + 1):
            source = me * blocks + b if i == 0 else adjacency[i - 1, me * blocks + b]
            owner = source // blocks
            if relative:
                owner = owner ^ me
                far = (owner // 4 + owner // 2 + owner) % 2
                place = (chips - owner // 2) % chips
                here, there = pieces[0][place], pieces[1][place]
                near, far = jnp.where(far == 0, here, there), jnp.where(far == 0, there, here)
                flips = [0] + [k for k in MEMBERS if k < total // members]
                parts = [
                    (near if k in (0,) + MERGE else far)[p * members : (p + 1) * members]
                    for p, k in enumerate(flips)
                ]
                found = jnp.concatenate(parts + [near[total:]], axis=0)
            else:
                found = pieces[0][owner]
            shift = ((i + blocks - source % blocks) % blocks) * OBS
            local = jnp.where(lane == i, pltpu.roll(found, shift, 1), local)
        pred, drawn = local[:total], local[total : total + members]
        own = local[:members] if relative else local[total + members : total + 2 * members]
        weight = local[rows - 8 : rows - 7]
        scaled = (pred - jnp.mean(pred, axis=0, keepdims=True)) * weight
        innov = (drawn - own) * weight
        both = jnp.concatenate(
            [scaled, innov, jnp.zeros((LOCAL - total - members, LOCAL), jnp.float32)], axis=0
        )
        matrix = lax.dot_general(
            scaled,
            both,
            (((1,), (1,)), ((), ())),
            precision=HIGHEST,
            preferred_element_type=jnp.float32,
        )
        row = lax.broadcasted_iota(jnp.int32, (total, LOCAL), 0)
        col = lax.broadcasted_iota(jnp.int32, (total, LOCAL), 1)
        systems.append(matrix + jnp.where(row == col, float(total - 1), 0.0))
    solved = solve(systems)
    for b in range(blocks):
        gain = solved[b] - jnp.mean(solved[b], axis=0, keepdims=True)
        gain_out[b] = jnp.transpose(gain)[total : total + members]


def find_gain(pieces, relative, index, adjacency, blocks, members, total):
    vmem = pl.BlockSpec(memory_space=pltpu.VMEM)
    smem = pl.BlockSpec(memory_space=pltpu.SMEM)
    return pl.pallas_call(
        functools.partial(gain_kernel, total, len(pieces), relative),
        out_shape=jax.ShapeDtypeStruct((blocks, members, total), jnp.float32),
        in_specs=[smem, smem] + [vmem] * len(pieces),
        out_specs=vmem,
        compiler_params=pltpu.CompilerParams(vmem_limit_bytes=VMEM_LIMIT),
        cost_estimate=pl.CostEstimate(flops=1, bytes_accessed=1, transcendentals=0),
        name="gain",
    )(index, adjacency, *pieces)


def carry_kernel(x, y):
    y[...] = x[...]


def carry(x, cost):
    vmem = pl.BlockSpec(memory_space=pltpu.VMEM)
    return pl.pallas_call(
        carry_kernel,
        out_shape=jax.ShapeDtypeStruct(x.shape, x.dtype),
        in_specs=[vmem],
        out_specs=vmem,
        compiler_params=pltpu.CompilerParams(vmem_limit_bytes=VMEM_LIMIT),
        cost_estimate=pl.CostEstimate(flops=cost, bytes_accessed=0, transcendentals=0),
        name="carry",
    )(x)


def store_kernel(flow, x, flow_hbm, y, sem):
    copy = pltpu.make_async_copy(flow, flow_hbm, sem)
    copy.start()
    y[...] = x[...]
    copy.wait()


def store(flow, x, cost):
    vmem = pl.BlockSpec(memory_space=pltpu.VMEM)
    return pl.pallas_call(
        store_kernel,
        out_shape=(
            jax.ShapeDtypeStruct(flow.shape, flow.dtype),
            jax.ShapeDtypeStruct(x.shape, x.dtype),
        ),
        in_specs=[vmem, vmem],
        out_specs=(pl.BlockSpec(memory_space=pltpu.HBM), vmem),
        scratch_shapes=[pltpu.SemaphoreType.DMA],
        compiler_params=pltpu.CompilerParams(vmem_limit_bytes=VMEM_LIMIT),
        cost_estimate=pl.CostEstimate(flops=cost, bytes_accessed=0, transcendentals=0),
        name="store",
    )(flow, x)


def update_kernel(gain, wet_own, dry, *refs):
    wets, (analysis_hbm, analysis, out_sems) = refs[:-3], refs[-3:]
    blocks = gain.shape[0]

    def out_copy(b):
        where = (slice(None), slice(None), pl.ds(b * NB, NB))
        return pltpu.make_async_copy(analysis.at[where], analysis_hbm.at[where], out_sems.at[b])

    tiles = dry.shape[2] // LOCAL
    for b in range(blocks):
        where = pl.ds(b * NB, NB)
        analysis[:, 0, where] = dry[0, :, where]
        analysis[:, 3, where] = dry[1, :, where]
        for k in range(2):
            at = k * tiles + b * NB // LOCAL
            spots = range(at, at + NB // LOCAL)

            def side(x):
                return jnp.concatenate([x[t] for t in spots], axis=1)

            if len(wets[0].shape) == 3:
                states = [side(wet_own)] + [side(w) for w in wets]
            else:
                states = [jnp.concatenate([w[:, t] for t in spots], axis=2).reshape(-1, NB) for w in wets]
            analysis[:, 1 + k, where] = side(wet_own) + jnp.dot(
                gain[b],
                jnp.concatenate(states, axis=0),
                precision=HIGHEST,
                preferred_element_type=jnp.float32,
            )
        out_copy(b).start()
    for b in range(blocks):
        out_copy(b).wait()


def update(gain, wet, dry, wets):
    _, members, width = dry.shape
    vmem = pl.BlockSpec(memory_space=pltpu.VMEM)
    return pl.pallas_call(
        update_kernel,
        out_shape=jax.ShapeDtypeStruct((members, 4, width), jnp.float32),
        in_specs=[vmem] * (3 + len(wets)),
        out_specs=pl.BlockSpec(memory_space=pltpu.HBM),
        scratch_shapes=[
            pltpu.VMEM((members, 4, width), jnp.float32),
            pltpu.SemaphoreType.DMA((width // NB,)),
        ],
        compiler_params=pltpu.CompilerParams(vmem_limit_bytes=VMEM_LIMIT),
        name="update",
    )(gain, wet, dry, *wets)


def permute(x, axis, mask):
    return lax.ppermute(x, axis, [(i, i ^ mask) for i in range(lax.axis_size(axis))])


def across(x, flip_member):
    basins, members = lax.axis_size("basin"), lax.axis_size("member")
    pairs = [
        (b * members + m, (b ^ 1) * members + (m ^ flip_member))
        for b in range(basins)
        for m in range(members)
    ]
    return lax.ppermute(x, ("basin", "member"), pairs)


def on_device(
    initial_reservoir_levels,
    normalized_catchment_settings,
    rainfall_member_series,
    surface_heat_celsius,
    potential_evapotranspiration,
    gauge_measured_values,
    gauge_deviation_sigma,
    gauge_perturbation_draws,
    gauge_catchment_position,
    gauge_present_flag,
    adjacent_block_list,
):
    members = rainfall_member_series.shape[1]
    blocks = gauge_measured_values.shape[0]
    basin_size, member_size = lax.axis_size("basin"), lax.axis_size("member")
    discharge, wet, dry, pred, fixed = forecast(
        initial_reservoir_levels,
        normalized_catchment_settings,
        rainfall_member_series,
        surface_heat_celsius,
        potential_evapotranspiration,
        gauge_measured_values,
        gauge_deviation_sigma,
        jnp.transpose(gauge_perturbation_draws, (0, 2, 1)),
        gauge_catchment_position,
        gauge_present_flag,
    )
    index = jnp.full((1,), lax.axis_index("basin"), jnp.int32)
    adjacency = jnp.transpose(adjacent_block_list)
    relative = basin_size <= 8 and member_size <= 4
    if relative:
        others = [k for k in MEMBERS if k < member_size]
        first = {k: permute(wet, "member", k) if k in MERGE else across(pred, k) for k in others}
        wets = [first[k] if k in MERGE else permute(wet, "member", k) for k in others]
        preds = [pred] + [first[k][-1] if k in MERGE else first[k] for k in others]
        near = jnp.concatenate(preds + [fixed], axis=0)[None]
        flips = [k for k in range(basin_size - 1, 1, -1) if k in (3, 5, 6)]
        near = jnp.concatenate([near] + [permute(near, "basin", k) for k in flips], axis=0)
        packs = [near, permute(near, "basin", 1)]
        discharge, dry = store(discharge, dry, COSTS[0])
        dry = carry(dry, COSTS[1])
    else:
        preds = lax.all_gather(pred, "member", axis=0).reshape(-1, LOCAL)
        wets = [lax.all_gather(wet, "member", axis=0)]
        mine = jnp.concatenate([preds, fixed[:members], pred, fixed[members:]], axis=0)
        packs = [lax.all_gather(mine, "basin", axis=0)]
    gain = find_gain(
        packs, relative, index, adjacency, blocks, members, members * member_size
    )
    analysis = update(gain, wet, dry, wets)
    return (analysis, discharge)


def solution(mesh):
    placed = (
        P("member", None, "basin"),
        P(None, "basin"),
        P(None, "member", "basin"),
        P(None, "basin"),
        P(None, "basin"),
        P("basin", None),
        P("basin", None),
        P("basin", None, "member"),
        P("basin", None),
        P("basin", None),
        P(),
    )
    return jax.shard_map(
        on_device,
        mesh=mesh,
        in_specs=placed,
        out_specs=(P("member", None, "basin"), P(None, "member", "basin")),
        check_vma=False,
    )
```
